32 devices in a mesh: grp: 8 (over z, core), head: 4 (over y, x).
Axes of the slice: x: 2, y: 2, z: 4, core: 2. Of those that a mesh axis runs over, the one named last changes fastest.
Arguments:
- query_rows: bfloat16 [32, 128, 2048], P(('grp', 'head')), may hold values from -6 to 6
- key_rows: bfloat16 [32, 128, 2048], P(('grp', 'head')), may hold values from -6 to 6
- value_rows: bfloat16 [32, 128, 2048], P(('grp', 'head')), may hold values from -6 to 6
- log_decay: bfloat16 [32, 128, 2048], P(('grp', 'head')), may hold values from -1.5 to 0, as said below
- beta_logit: bfloat16 [32, 128, 16], P(('grp', 'head')), may hold values from -6 to 6
- out_grad: bfloat16 [32, 128, 2048], P(('grp', 'head')), may hold values from -6 to 6
- fork_state: float32 [8, 16, 128, 128], P(None, 'head'), may hold values from -6 to 6
- branch_prompt: int32 [32], replicated, may hold values from 0 to 7, as said below
- valid_len: int32 [32], replicated, may hold values from 32 to 128, as said below
Outputs:
- grad_query: bfloat16 [32, 128, 2048], P(('grp', 'head'))
- grad_key: bfloat16 [32, 128, 2048], P(('grp', 'head'))
- grad_value: bfloat16 [32, 128, 2048], P(('grp', 'head'))
- grad_decay: bfloat16 [32, 128, 2048], P(('grp', 'head'))
- grad_beta: bfloat16 [32, 128, 16], P(('grp', 'head'))
- grad_fork: float32 [8, 16, 128, 128], P(None, 'head')
The draws below stay inside these ranges and needn't reach their ends.
Inputs may be any that keep to these rules, and one draw needn't show every extreme that they name: `log_decay`: never positive; a few tokens of each branch lose a large share of every channel at once. `branch_prompt`: every prompt has at least one branch. A branch counts its first valid_len tokens; some branch uses all 128.
All inputs are finite; a program needn't handle non-finite values.
Results may differ from the reference program's by a relative error of at most 0.0015.
Values may be sent and summed in bfloat16 or wider, within the bound.
No kernel may reach another device: no remote copies, remote signals or barrier semaphores. Data moves between devices by JAX's collectives and lax.ppermute only.
A program may use at most 64 MiB of HBM per device.

```python
import math
import jax
import jax.numpy as jnp
from jax import lax

HEADS = 16
HEAD_DIM = 128
WINDOW_TOKENS = 128
PROMPTS = 8
BRANCH_TOTAL = 32


def draw_log_decay(key, part):
    random_subkeys = jax.random.split(jax.random.fold_in(key, 11), 5)
    channels = HEADS * HEAD_DIM
    channel_decay_rate = jnp.exp(jax.random.uniform(random_subkeys[0], (channels,), jnp.float32, math.log(0.2 / WINDOW_TOKENS), math.log(0.04)))
    branch_factor = jnp.exp(jax.random.uniform(random_subkeys[1], (BRANCH_TOTAL, 1, 1), jnp.float32, math.log(0.5), math.log(2.0)))
    random_noise = jnp.exp(jax.random.uniform(random_subkeys[2], (BRANCH_TOTAL, WINDOW_TOKENS, channels), jnp.float32, math.log(0.5), math.log(2.0)))
    spike_position = jax.random.randint(random_subkeys[3], (BRANCH_TOTAL, 3), 0, WINDOW_TOKENS)
    spike_strength = jax.random.uniform(random_subkeys[4], (BRANCH_TOTAL, 3), jnp.float32, math.log(0.5), math.log(0.8))
    token_positions = jnp.arange(WINDOW_TOKENS, dtype=jnp.int32)
    spike_event = jnp.sum(jnp.where(token_positions[None, :, None] == spike_position[:, None, :], spike_strength[:, None, :], 0.0), axis=-1)
    output_values = -channel_decay_rate[None, None, :] * branch_factor * random_noise + spike_event[:, :, None]
    return output_values.astype(jnp.bfloat16)


def draw_branch_prompt(key, part):
    random_subkeys = jax.random.split(jax.random.fold_in(key, 23), 2)
    chosen = jax.random.randint(random_subkeys[0], (BRANCH_TOTAL,), 0, PROMPTS)
    spots = jax.random.permutation(random_subkeys[1], BRANCH_TOTAL)[:PROMPTS]
    return chosen.at[spots].set(jnp.arange(PROMPTS, dtype=jnp.int32)).astype(jnp.int32)


def draw_valid_len(key, part):
    random_subkeys = jax.random.split(jax.random.fold_in(key, 37), 2)
    lengths_out = jax.random.randint(random_subkeys[0], (BRANCH_TOTAL,), WINDOW_TOKENS // 4, WINDOW_TOKENS + 1)
    spot = jax.random.randint(random_subkeys[1], (), 0, BRANCH_TOTAL)
    return lengths_out.at[spot].set(WINDOW_TOKENS).astype(jnp.int32)


def level_of(rng, dims, shards, smallest, top_value):
    level = 1.0
    for axis_at, blocks in shards:
        heights = jax.random.uniform(jax.random.fold_in(jax.random.fold_in(rng, 6), axis_at), (blocks,), jnp.float32, smallest / len(shards), top_value / len(shards))
        level = level * jnp.repeat(jnp.exp(heights), dims[axis_at] // blocks).reshape((-1,) + (1,) * (len(dims) - 1 - axis_at))
    return level


def scatter_about(key, dims, scale, reach, cuts=(), kind=jnp.bfloat16):
    result = jax.random.normal(key, dims, jnp.float32) * scale
    if len(cuts) > 0:
        result = level_of(key, dims, cuts, -0.22, 0.18) * result
    return jnp.clip(result, min=-reach, max=reach).astype(kind)


def setup_inputs(seed: int = 0) -> dict:
    arg_keys = jax.random.split(jax.random.key(seed), 10)
    return {
        "query_rows": scatter_about(arg_keys[0], (BRANCH_TOTAL, WINDOW_TOKENS, HEADS * HEAD_DIM), 1.0, 6.0, ((0, 32),)),
        "key_rows": scatter_about(arg_keys[1], (BRANCH_TOTAL, WINDOW_TOKENS, HEADS * HEAD_DIM), 1.0, 6.0, ((0, 32),)),
        "value_rows": scatter_about(arg_keys[2], (BRANCH_TOTAL, WINDOW_TOKENS, HEADS * HEAD_DIM), 1.0, 6.0, ((0, 32),)),
        "log_decay": draw_log_decay(jax.random.fold_in(arg_keys[9], 71), 0),
        "beta_logit": scatter_about(arg_keys[4], (BRANCH_TOTAL, WINDOW_TOKENS, HEADS), 1.5, 6.0, ((0, 32),)),
        "out_grad": scatter_about(arg_keys[5], (BRANCH_TOTAL, WINDOW_TOKENS, HEADS * HEAD_DIM), 1.0, 6.0, ((0, 32),)),
        "fork_state": scatter_about(arg_keys[6], (PROMPTS, HEADS, HEAD_DIM, HEAD_DIM), 1.0, 6.0, ((1, 4),), jnp.float32),
        "branch_prompt": draw_branch_prompt(jax.random.fold_in(arg_keys[9], 71), 0),
        "valid_len": draw_valid_len(jax.random.fold_in(arg_keys[9], 71), 0),
    }


def decay_forward(query_in, key_in, value_in, decay_in, beta_in, state_in, keep_mask, block_len):
    head_dim = query_in.shape[-1]
    window_len = query_in.shape[1]
    upper_limit = lax.Precision.HIGHEST
    unit_query = query_in * lax.rsqrt(lax.optimization_barrier(jnp.sum(query_in * query_in, axis=-1, keepdims=True)) + 1e-06) * head_dim ** (-0.5)
    unit_key = key_in * lax.rsqrt(lax.optimization_barrier(jnp.sum(key_in * key_in, axis=-1, keepdims=True)) + 1e-06)
    beta_value = jax.nn.sigmoid(beta_in) * keep_mask[None, :]
    decay_value = decay_in * keep_mask[None, :, None]
    token_positions = jnp.arange(block_len, dtype=jnp.int32)
    lower_strict = (token_positions[:, None] > token_positions[None, :]).astype(jnp.float32)
    lower_closed = (token_positions[:, None] >= token_positions[None, :]).astype(jnp.float32)
    identity_block = jnp.eye(block_len, dtype=jnp.float32)
    outputs = []
    current_state = state_in
    for block_index in range(window_len // block_len):
        first_pos = block_index * block_len
        cum_decay = jnp.cumsum(decay_value[:, first_pos:first_pos + block_len], axis=1)
        growth = jnp.exp(cum_decay)
        shrink = jnp.exp(-cum_decay)
        key_block = unit_key[:, first_pos:first_pos + block_len]
        query_block = unit_query[:, first_pos:first_pos + block_len]
        block_value_rows = value_in[:, first_pos:first_pos + block_len]
        block_beta_rows = beta_value[:, first_pos:first_pos + block_len]
        key_forward_rows = key_block * growth
        key_earlier_rows = key_block * shrink
        query_forward_rows = query_block * growth
        coupling = jnp.einsum('htk,hsk->hts', key_forward_rows, key_earlier_rows, precision=upper_limit) * block_beta_rows[:, :, None] * lower_strict
        attend_scores = jnp.einsum('htk,hsk->hts', query_forward_rows, key_earlier_rows, precision=upper_limit) * lower_closed
        target_output = block_beta_rows[:, :, None] * (block_value_rows - jnp.einsum('led,ldf->lef', key_forward_rows, current_state, precision=upper_limit))
        state_update = jax.scipy.linalg.solve_triangular(identity_block + coupling, target_output, lower=True, unit_diagonal=True)
        output_block_rows = jnp.einsum('led,ldf->lef', query_forward_rows, current_state, precision=upper_limit) + jnp.einsum('ifj,ijo->ifo', attend_scores, state_update, precision=upper_limit)
        tail_increase = growth[:, -1, :]
        current_state = tail_increase[:, :, None] * current_state + jnp.einsum('lei,leg->lig', key_earlier_rows * tail_increase[:, None, :], state_update, precision=upper_limit)
        outputs.append(output_block_rows)
    return jnp.concatenate(outputs, axis=1)

def reference(query_rows, key_rows, value_rows, log_decay, beta_logit, out_grad, fork_state, branch_prompt, valid_len):
    block_len = min(64, WINDOW_TOKENS)

    def one_branch(fork_total, branch_index):

        def pick_branch(array_in):
            return lax.dynamic_index_in_dim(array_in, branch_index, 0, keepdims=False)

        def split_heads(array_in):
            return pick_branch(array_in).astype(jnp.float32).reshape(WINDOW_TOKENS, HEADS, HEAD_DIM).transpose(1, 0, 2)

        def join_heads(array_in):
            return array_in.transpose(1, 0, 2).reshape(WINDOW_TOKENS, HEADS * HEAD_DIM).astype(jnp.bfloat16)
        prompt_id = pick_branch(branch_prompt)
        keep_mask = (jnp.arange(WINDOW_TOKENS, dtype=jnp.int32) < pick_branch(valid_len)).astype(jnp.float32)
        state_in = lax.dynamic_index_in_dim(fork_state, prompt_id, 0, keepdims=False)
        beta_in = pick_branch(beta_logit).astype(jnp.float32).T

        def forward_one(query_in, key_in, value_in, decay_in, beta_one, state_one):
            return decay_forward(query_in, key_in, value_in, decay_in, beta_one, state_one, keep_mask, block_len)
        outputs, pullback = jax.vjp(forward_one, split_heads(query_rows), split_heads(key_rows), split_heads(value_rows), split_heads(log_decay), beta_in, state_in)
        cotangent = split_heads(out_grad) * keep_mask[None, :, None]
        grad_q, grad_k, grad_v, grad_g, grad_b, grad_s = pullback(cotangent)
        previous = lax.dynamic_index_in_dim(fork_total, prompt_id, 0, keepdims=False)
        fork_total = lax.dynamic_update_index_in_dim(fork_total, previous + grad_s, prompt_id, 0)
        return (fork_total, (join_heads(grad_q), join_heads(grad_k), join_heads(grad_v), join_heads(grad_g), grad_b.T.astype(jnp.bfloat16)))
    start_total = jnp.zeros((PROMPTS, HEADS, HEAD_DIM, HEAD_DIM), jnp.float32)
    fork_total, per_branch = lax.scan(one_branch, start_total, jnp.arange(BRANCH_TOTAL, dtype=jnp.int32))
    return (per_branch[0], per_branch[1], per_branch[2], per_branch[3], per_branch[4], fork_total)
```

```python
import functools

import jax
import jax.numpy as jnp
from jax import lax
from jax.experimental import pallas as pl
from jax.experimental.pallas import tpu as pltpu
from jax.sharding import PartitionSpec as P

HIGH = lax.Precision.HIGH
NN = ((1,), (0,))
NT = ((1,), (1,))
TN = ((0,), (0,))
F32 = jnp.float32
BF16 = jnp.bfloat16


def dot(a, b, dims=NN, precision=None):
    return lax.dot_general(
        a, b, (dims, ((), ())), preferred_element_type=F32, precision=precision
    )


def split(x):
    high = x.astype(BF16)
    return high, (x - high.astype(F32)).astype(BF16)


def encode(x):
    return (x * x * x * jnp.abs(x)).astype(BF16)


def decode(y):
    wide = y.astype(F32)
    root = jnp.sqrt(jnp.sqrt(jnp.abs(wide)))
    return jnp.where(wide < 0, -root, root)


def iota2(shape, axis):
    return lax.broadcasted_iota(jnp.int32, shape, axis)


def unit_lower_inverse(matrices):
    size = matrices[0].shape[0]
    blocks = size // 8
    row, col = iota2((size, size), 0), iota2((size, size), 1)
    on_block = row // 8 == col // 8
    lane8 = iota2((8, size), 1)
    identity8 = (iota2((8, size), 0) == lane8 % 8).astype(F32)
    inverses = []
    for a in matrices:
        compact = jnp.sum(jnp.where(on_block, a, 0.0).reshape(blocks, 8, size), axis=0)
        inverse = identity8
        for m in range(7):
            column = jnp.take_along_axis(compact, lane8 // 8 * 8 + m, axis=1)
            inverse = inverse - column * inverse[m : m + 1]
        inverses.append(jnp.where(on_block, jnp.concatenate([inverse] * blocks, axis=0), 0.0))
    width = 8
    while width * 2 < size:
        lower = (row // (2 * width) == col // (2 * width)) & (row // width > col // width)
        inner = [
            dot(jnp.where(lower, a, 0.0), d, precision=HIGH) for a, d in zip(matrices, inverses)
        ]
        inverses = [d - dot(d, x, precision=HIGH) for d, x in zip(inverses, inner)]
        width *= 2
    results = []
    inner = [
        dot(a[width:, :width], d[:width, :width], precision=HIGH)
        for a, d in zip(matrices, inverses)
    ]
    corner = [dot(d[width:, width:], x, precision=HIGH) for d, x in zip(inverses, inner)]
    for d, x in zip(inverses, corner):
        bottom = jnp.concatenate([-x, d[width:, width:]], axis=1)
        results.append(jnp.concatenate([d[:width], bottom], axis=0))
    return results


def decayed_rows(query_in, key_in, decay_in, valid, tri):
    tokens, head_dim = query_in.shape
    row = iota2((tokens, 1), 0)
    query = query_in.astype(F32)
    key = key_in.astype(F32)
    query_scale = lax.rsqrt(jnp.sum(query * query, axis=1, keepdims=True) + 1e-06)
    key_scale = lax.rsqrt(jnp.sum(key * key, axis=1, keepdims=True) + 1e-06)
    unit_query = query * query_scale
    unit_key = key * key_scale
    decay = jnp.where(row < valid, decay_in, jnp.zeros_like(decay_in))
    cumulative = dot(tri, decay)
    middle = cumulative[tokens // 2 - 1 : tokens // 2]
    cumulative = cumulative - middle
    grow = jnp.exp(cumulative)
    shrink = jnp.exp(-cumulative)
    return dict(
        unit_query=unit_query,
        unit_key=unit_key,
        query_scale=query_scale,
        key_scale=key_scale,
        grow=grow,
        shrink=shrink,
        start=jnp.exp(middle),
        key_forward=unit_key * grow,
        key_earlier=unit_key * shrink,
        query_forward=unit_query * (grow * head_dim**-0.5),
    )


def head_column(values, head):
    lane = iota2(values.shape, 1)
    return jnp.sum(jnp.where(lane == head, values, 0.0), axis=1, keepdims=True)


def first_kernel(
    per_step,
    valid_ref,
    query_ref,
    key_ref,
    decay_ref,
    grad_ref,
    beta_ref,
    value_grad_ref,
    wide_ref,
    inverse_ref,
    coded_ref,
):
    tokens = query_ref.shape[1]
    head_dim = query_ref.shape[2] // per_step
    pieces = coded_ref.shape[0]
    valid = valid_ref[pl.program_id(0)]
    row, col = iota2((tokens, tokens), 0), iota2((tokens, tokens), 1)
    tri = (row >= col).astype(BF16)
    keep = iota2((tokens, 1), 0) < valid
    betas = jax.nn.sigmoid(beta_ref[0].astype(F32)) * keep.astype(F32)
    rows, beta, out_grad = [], [], []
    for j in range(per_step):
        lanes = slice(j * head_dim, (j + 1) * head_dim)
        rows.append(
            decayed_rows(
                query_ref[0, :, lanes], key_ref[0, :, lanes], decay_ref[0, :, lanes], valid, tri
            )
        )
        beta.append(head_column(betas, pl.program_id(1) * per_step + j))
        grad = grad_ref[0, :, lanes]
        out_grad.append(jnp.where(keep, grad, jnp.zeros_like(grad)))
    scores = [
        dot(
            jnp.concatenate([r["key_forward"], r["query_forward"]], axis=0),
            r["key_earlier"],
            NT,
            HIGH,
        )
        for r in rows
    ]
    coupling = [jnp.where(row > col, s[:tokens], 0.0) * b for s, b in zip(scores, beta)]
    attend = [jnp.where(row >= col, s[tokens:], 0.0) for s in scores]
    inverse = unit_lower_inverse(coupling)
    update_grad = []
    for p, g in zip(attend, out_grad):
        high, low = split(p)
        update_grad.append(dot(high, g, TN) + dot(low, g, TN))
    value_grad = [b * dot(d, u, TN, HIGH) for b, d, u in zip(beta, inverse, update_grad)]
    for j in range(per_step):
        r = rows[j]
        high, low = split(r["query_forward"] * r["start"])
        state_grad = (
            dot(high, out_grad[j], TN)
            + dot(low, out_grad[j], TN)
            - dot(r["key_forward"] * r["start"], value_grad[j], TN, HIGH)
        )
        coded_ref[:, j] = encode(state_grad).reshape(pieces, head_dim // pieces, head_dim)
        lanes = slice(j * head_dim, (j + 1) * head_dim)
        value_grad_ref[0, :, lanes] = value_grad[j].astype(BF16)
        wide_ref[0, j] = value_grad[j]
        inverse_ref[0, j] = inverse[j]


def second_kernel(
    per_step,
    valid_ref,
    query_ref,
    key_ref,
    value_ref,
    decay_ref,
    grad_ref,
    beta_ref,
    wide_ref,
    inverse_ref,
    state_ref,
    query_grad_ref,
    key_grad_ref,
    decay_grad_ref,
    beta_grad_ref,
):
    tokens = query_ref.shape[1]
    head_dim = query_ref.shape[2] // per_step
    valid = valid_ref[pl.program_id(0)]
    row, col = iota2((tokens, tokens), 0), iota2((tokens, tokens), 1)
    tri = (row >= col).astype(BF16)
    keep = iota2((tokens, 1), 0) < valid
    logits = beta_ref[0].astype(F32)
    betas = jax.nn.sigmoid(logits) * keep.astype(F32)
    ratios = jnp.exp(-logits)
    beta_grad = jnp.zeros(logits.shape, F32)
    heads = range(per_step)
    lanes = [slice(j * head_dim, (j + 1) * head_dim) for j in heads]
    number = [pl.program_id(1) * per_step + j for j in heads]
    rows = [
        decayed_rows(
            query_ref[0, :, lanes[j]],
            key_ref[0, :, lanes[j]],
            decay_ref[0, :, lanes[j]],
            valid,
            tri,
        )
        for j in heads
    ]
    beta = [head_column(betas, n) for n in number]
    target = [
        value_ref[0, :, lanes[j]].astype(F32)
        - dot(rows[j]["key_forward"] * rows[j]["start"], state_ref[j], precision=HIGH)
        for j in heads
    ]
    update = [dot(inverse_ref[0, j], beta[j] * target[j], precision=HIGH) for j in heads]
    wide = [wide_ref[0, j] for j in heads]
    both = []
    for j in heads:
        grad = grad_ref[0, :, lanes[j]]
        grad = jnp.where(keep, grad, jnp.zeros_like(grad)).astype(F32)
        both.append(jnp.concatenate([grad, -wide[j]], axis=0))
    score_grad = [dot(both[j], update[j], NT, HIGH) for j in heads]
    attend_grad = [jnp.where(row >= col, s[:tokens], 0.0) for s in score_grad]
    coupling_grad = [jnp.where(row > col, s[tokens:], 0.0) for s in score_grad]
    for j in heads:
        r = rows[j]
        through_state = dot(both[j], state_ref[j], NT, HIGH) * r["start"]
        through_rows = dot(
            jnp.concatenate([attend_grad[j], coupling_grad[j]], axis=0),
            r["key_earlier"],
            precision=HIGH,
        )
        forward = through_state + through_rows
        earlier = dot(
            jnp.concatenate([attend_grad[j], coupling_grad[j]], axis=0),
            jnp.concatenate([r["query_forward"], r["key_forward"]], axis=0),
            TN,
            HIGH,
        )
        query_unit_grad = forward[:tokens] * r["grow"] * head_dim**-0.5
        key_later = forward[tokens:] * r["grow"]
        key_before = earlier * r["shrink"]
        key_unit_grad = key_later + key_before
        decay_step = r["unit_query"] * query_unit_grad + r["unit_key"] * (key_later - key_before)
        high, low = split(decay_step)
        decay_grad = dot(tri, high, TN) + dot(tri, low, TN)
        decay_grad_ref[0, :, lanes[j]] = jnp.where(keep, decay_grad, 0.0).astype(BF16)
        along = jnp.sum(r["unit_query"] * query_unit_grad, axis=1, keepdims=True)
        query_grad_ref[0, :, lanes[j]] = (
            r["query_scale"] * (query_unit_grad - r["unit_query"] * along)
        ).astype(BF16)
        along = jnp.sum(r["unit_key"] * key_unit_grad, axis=1, keepdims=True)
        key_grad_ref[0, :, lanes[j]] = (
            r["key_scale"] * (key_unit_grad - r["unit_key"] * along)
        ).astype(BF16)
        strength = jnp.sum(wide[j] * update[j], axis=1, keepdims=True)
        beta_grad = jnp.where(iota2(logits.shape, 1) == number[j], strength * ratios, beta_grad)

    @pl.when(pl.program_id(1) == 0)
    def _():
        beta_grad_ref[0] = beta_grad.astype(BF16)

    @pl.when(pl.program_id(1) > 0)
    def _():
        beta_grad_ref[0] = (beta_grad_ref[0].astype(F32) + beta_grad).astype(BF16)


def sum_kernel(prompt_ref, coded_ref, out_ref, total_ref):
    total_ref[...] = jnp.zeros_like(total_ref)

    def add(branch, carry):
        prompt = prompt_ref[branch]
        total_ref[prompt] += decode(coded_ref[branch])
        return carry

    lax.fori_loop(0, coded_ref.shape[0], add, 0)
    out_ref[...] = encode(total_ref[...])


def spread_kernel(place_ref, *refs):
    out_ref = refs[-1]
    for i, piece in enumerate(refs[:-1]):
        out_ref[:, :, pl.ds(place_ref[i], 1)] = decode(piece[...])[:, :, None]


def gather_pieces(piece, axis_name):
    size = lax.axis_size(axis_name)
    me = lax.axis_index(axis_name)
    pieces, places = [piece], [me]
    chips = size // 2
    power = chips & (chips - 1) == 0
    for step in range(1, chips):
        other = [((c ^ step) if power else (c + step) % chips) for c in range(chips)]
        moves = [(2 * c + core, 2 * other[c] + core) for c in range(chips) for core in range(2)]
        pieces.append(lax.ppermute(piece, axis_name, moves))
        chip = me // 2
        source = (chip ^ step) if power else (chip - step) % chips
        places.append(2 * source + me % 2)
    swap = [(i, i ^ 1) for i in range(size)]
    swapped = [lax.ppermute(x, axis_name, swap) for x in pieces]
    return pieces + swapped, places + [p ^ 1 for p in places]


def per_device(
    query_rows,
    key_rows,
    value_rows,
    log_decay,
    beta_logit,
    out_grad,
    fork_state,
    branch_prompt,
    valid_len,
):
    count, tokens, width = query_rows.shape
    prompts, heads_here, head_dim, _ = fork_state.shape
    members = lax.axis_size("head")
    groups = lax.axis_size("grp")
    heads = members * heads_here
    piece_rows = head_dim // groups
    first_branch = (lax.axis_index("grp") * members + lax.axis_index("head")) * count
    valid = lax.dynamic_slice_in_dim(valid_len, first_branch, count)
    group_prompt = lax.dynamic_slice_in_dim(
        branch_prompt, lax.axis_index("grp") * members * count, members * count
    )
    chosen = jnp.take(fork_state, group_prompt, axis=0)
    states = lax.all_to_all(
        chosen.reshape(members, count * heads_here, head_dim, head_dim), "head", 0, 0, tiled=True
    )
    states = (
        states.reshape(members, count, heads_here, head_dim, head_dim)
        .transpose(1, 0, 2, 3, 4)
        .reshape(count * heads, head_dim, head_dim)
    )

    per_step = next(n for n in (4, 2, 1) if heads % n == 0)
    steps = heads // per_step
    row_block = pl.BlockSpec((1, tokens, per_step * head_dim), lambda b, i, *_: (b, 0, i))
    beta_block = pl.BlockSpec((1, tokens, heads), lambda b, i, *_: (b, 0, 0))
    square_block = pl.BlockSpec((1, per_step, tokens, tokens), lambda b, i, *_: (b, i, 0, 0))
    wide_block = pl.BlockSpec((1, per_step, tokens, head_dim), lambda b, i, *_: (b, i, 0, 0))
    params = pltpu.CompilerParams(vmem_limit_bytes=48 * 2**20)
    rows_type = jax.ShapeDtypeStruct(query_rows.shape, BF16)
    units = count * heads * tokens * tokens * head_dim

    value_grad, wide, inverse, coded = pl.pallas_call(
        functools.partial(first_kernel, per_step),
        grid_spec=pltpu.PrefetchScalarGridSpec(
            num_scalar_prefetch=1,
            grid=(count, steps),
            in_specs=[row_block, row_block, row_block, row_block, beta_block],
            out_specs=[
                row_block,
                wide_block,
                square_block,
                pl.BlockSpec(
                    (groups, per_step, piece_rows, head_dim),
                    lambda b, i, *_: (0, b * steps + i, 0, 0),
                ),
            ],
        ),
        out_shape=[
            rows_type,
            jax.ShapeDtypeStruct((count, heads, tokens, head_dim), F32),
            jax.ShapeDtypeStruct((count, heads, tokens, tokens), F32),
            jax.ShapeDtypeStruct((groups, count * heads, piece_rows, head_dim), BF16),
        ],
        compiler_params=params,
        cost_estimate=pl.CostEstimate(flops=80 * units, bytes_accessed=2**23, transcendentals=0),
        name="state_independent",
    )(valid, query_rows, key_rows, log_decay, out_grad, beta_logit)

    coded = (
        coded.reshape(groups, count, members, heads_here, piece_rows, head_dim)
        .transpose(0, 2, 1, 3, 4, 5)
        .reshape(groups * members, count, heads_here, piece_rows, head_dim)
    )
    arrived = lax.all_to_all(coded, ("grp", "head"), 0, 0, tiled=True)

    query_grad, key_grad, decay_grad, beta_grad = pl.pallas_call(
        functools.partial(second_kernel, per_step),
        grid_spec=pltpu.PrefetchScalarGridSpec(
            num_scalar_prefetch=1,
            grid=(count, steps),
            in_specs=[
                row_block,
                row_block,
                row_block,
                row_block,
                row_block,
                beta_block,
                wide_block,
                square_block,
                pl.BlockSpec(
                    (per_step, head_dim, head_dim), lambda b, i, *_: (b * steps + i, 0, 0)
                ),
            ],
            out_specs=[row_block, row_block, row_block, beta_block],
        ),
        out_shape=[
            rows_type,
            rows_type,
            rows_type,
            jax.ShapeDtypeStruct(beta_logit.shape, BF16),
        ],
        compiler_params=params,
        cost_estimate=pl.CostEstimate(flops=80 * units, bytes_accessed=2**23, transcendentals=0),
        name="state_dependent",
    )(
        valid,
        query_rows,
        key_rows,
        value_rows,
        log_decay,
        out_grad,
        beta_logit,
        wide,
        inverse,
        states,
    )

    piece_shape = (prompts, heads_here, piece_rows, head_dim)
    branches = groups * members * count
    whole = pl.BlockSpec(memory_space=pltpu.VMEM)
    scalars = pl.BlockSpec(memory_space=pltpu.SMEM)
    piece = pl.pallas_call(
        sum_kernel,
        in_specs=[scalars, whole],
        out_specs=whole,
        out_shape=jax.ShapeDtypeStruct(piece_shape, BF16),
        scratch_shapes=[pltpu.VMEM(piece_shape, F32)],
        compiler_params=params,
        name="sum_by_prompt",
    )(branch_prompt, arrived.reshape(branches, heads_here, piece_rows, head_dim))
    pieces, places = gather_pieces(piece, "grp")
    grad_fork = pl.pallas_call(
        spread_kernel,
        in_specs=[scalars] + [whole] * len(pieces),
        out_specs=whole,
        out_shape=jax.ShapeDtypeStruct(
            (prompts, heads_here, groups, piece_rows, head_dim), F32
        ),
        compiler_params=params,
        name="spread_pieces",
    )(jnp.stack(places).astype(jnp.int32), *pieces)
    return (
        query_grad,
        key_grad,
        value_grad,
        decay_grad,
        beta_grad,
        grad_fork.reshape(fork_state.shape),
    )


def solution(mesh):
    rows = P(("grp", "head"), None, None)
    state = P(None, "head", None, None)
    return jax.shard_map(
        per_device,
        mesh=mesh,
        in_specs=(rows, rows, rows, rows, rows, rows, state, P(), P()),
        out_specs=(rows, rows, rows, rows, rows, state),
        check_vma=False,
    )
```

```python
import functools

import jax
import jax.numpy as jnp
from jax import lax
from jax.experimental import pallas as pl
from jax.experimental.pallas import tpu as pltpu
from jax.sharding import PartitionSpec as P

HIGH = lax.Precision.HIGH
NN = ((1,), (0,))
NT = ((1,), (1,))
TN = ((0,), (0,))
F32 = jnp.float32
BF16 = jnp.bfloat16


def dot(a, b, dims=NN, precision=None):
    return lax.dot_general(
        a, b, (dims, ((), ())), preferred_element_type=F32, precision=precision
    )


def split(x):
    high = x.astype(BF16)
    return high, (x - high.astype(F32)).astype(BF16)


def encode(x):
    return (x * x * x * jnp.abs(x)).astype(BF16)


def decode(y):
    wide = y.astype(F32)
    root = lax.rsqrt(lax.rsqrt(jnp.abs(wide)))
    return jnp.where(wide < 0, -root, root)


def iota2(shape, axis):
    return lax.broadcasted_iota(jnp.int32, shape, axis)


def dot3(a, b):
    return dot(a[0], b[0]) + dot(a[1], b[0]) + dot(a[0], b[1])


def stack(a, b, axis):
    return tuple(jnp.concatenate([x, y], axis=axis) for x, y in zip(a, b))


def unit_upper_inverse(matrices, width):
    size = matrices[0].shape[0]
    blocks = size // width
    row, col = iota2((size, size), 0), iota2((size, size), 1)
    on_block = row // width == col // width
    lane = iota2((8, size), 1)
    identity = (iota2((width, size), 0) == iota2((width, size), 1) % width).astype(F32)
    inverses = []
    for a in matrices:
        compact = jnp.sum(jnp.where(on_block, a, 0.0).reshape(blocks, width, size), axis=0)
        slabs = [compact[i : i + 8] for i in range(0, width, 8)]
        result = [identity[i : i + 8] for i in range(0, width, 8)]
        for m in reversed(range(1, width)):
            source = result[m // 8][m % 8 : m % 8 + 1]
            for i in range((m - 1) // 8 + 1):
                column = jnp.take_along_axis(slabs[i], lane // width * width + m, axis=1)
                result[i] = result[i] - column * source
        inverses.append(jnp.where(on_block, jnp.concatenate(result * blocks, axis=0), 0.0))
    while width * 2 < size:
        upper = (row // (2 * width) == col // (2 * width)) & (row // width < col // width)
        parts = [split(d) for d in inverses]
        inner = [dot3(split(jnp.where(upper, a, 0.0)), d) for a, d in zip(matrices, parts)]
        inverses = [d - dot3(p, split(x)) for d, p, x in zip(inverses, parts, inner)]
        width *= 2
    results = []
    first = [split(d[:width, :width]) for d in inverses]
    second = [split(d[width:, width:]) for d in inverses]
    inner = [dot3(split(a[:width, width:]), d) for a, d in zip(matrices, second)]
    corner = [dot3(d, split(x)) for d, x in zip(first, inner)]
    for d, x in zip(inverses, corner):
        top = jnp.concatenate([d[:width, :width], -x], axis=1)
        results.append(jnp.concatenate([top, d[width:]], axis=0))
    return results


def decayed_rows(query_in, key_in, decay_in, valid, tri):
    tokens, head_dim = query_in.shape
    row = iota2((tokens, 1), 0)
    query = query_in.astype(F32)
    key = key_in.astype(F32)
    query_scale = lax.rsqrt(jnp.sum(query * query, axis=1, keepdims=True) + 1e-06)
    key_scale = lax.rsqrt(jnp.sum(key * key, axis=1, keepdims=True) + 1e-06)
    unit_query = query * query_scale
    unit_key = key * key_scale
    decay = jnp.where(row < valid, decay_in, jnp.zeros_like(decay_in))
    cumulative = dot(tri, decay)
    middle = cumulative[tokens // 2 - 1 : tokens // 2]
    cumulative = cumulative - middle
    grow = jnp.exp(cumulative)
    shrink = jnp.exp(-cumulative)
    return dict(
        unit_query=unit_query,
        unit_key=unit_key,
        query_scale=query_scale,
        key_scale=key_scale,
        grow=grow,
        shrink=shrink,
        start=jnp.exp(middle),
        key_forward=unit_key * grow,
        key_earlier=unit_key * shrink,
        query_forward=unit_query * (grow * head_dim**-0.5),
    )


def head_column(values, head):
    lane = iota2(values.shape, 1)
    return jnp.sum(jnp.where(lane == head, values, 0.0), axis=1, keepdims=True)


def own_branch(count):
    place = lax.axis_index("grp") * lax.axis_size("head") + lax.axis_index("head")
    return place * count


def first_kernel(
    per_step,
    width,
    valid_ref,
    query_ref,
    key_ref,
    decay_ref,
    grad_ref,
    beta_ref,
    value_grad_ref,
    value_low_ref,
    inverse_ref,
    coded_ref,
):
    tokens = query_ref.shape[1]
    head_dim = query_ref.shape[2] // per_step
    pieces = coded_ref.shape[0]
    valid = valid_ref[own_branch(pl.num_programs(0)) + pl.program_id(0)]
    row, col = iota2((tokens, tokens), 0), iota2((tokens, tokens), 1)
    tri = (row >= col).astype(BF16)
    keep = iota2((tokens, 1), 0) < valid
    lane_keep = iota2((1, tokens), 1) < valid
    flat_betas = jax.nn.sigmoid(beta_ref[0].astype(F32)) * lane_keep.astype(F32)
    betas = flat_betas.T
    heads = range(per_step)
    lanes = [slice(j * head_dim, (j + 1) * head_dim) for j in heads]
    number = [pl.program_id(1) * per_step + j for j in heads]
    rows = [
        decayed_rows(
            query_ref[0, :, lanes[j]], key_ref[0, :, lanes[j]], decay_ref[0, :, lanes[j]], valid, tri
        )
        for j in heads
    ]
    beta = [head_column(betas, n) for n in number]
    flat_beta = [
        jnp.sum(
            jnp.where(iota2(flat_betas.shape, 0) == n, flat_betas, 0.0), axis=0, keepdims=True
        )
        for n in number
    ]
    out_grad = []
    for j in heads:
        grad = grad_ref[0, :, lanes[j]]
        out_grad.append(jnp.where(keep, grad, jnp.zeros_like(grad)))
    across = [
        split(jnp.concatenate([r["key_forward"], r["query_forward"]], axis=0).T) for r in rows
    ]
    scores = [dot3(split(r["key_earlier"]), x) for r, x in zip(rows, across)]
    coupling = [
        jnp.where(row < col, s[:, :tokens] * b, 0.0) for s, b in zip(scores, flat_beta)
    ]
    attend = [split(jnp.where(row <= col, s[:, tokens:], 0.0)) for s in scores]
    inverse = [split(x) for x in unit_upper_inverse(coupling, width)]
    update_grad = [
        split(dot(p[0], g) + dot(p[1], g)) for p, g in zip(attend, out_grad)
    ]
    value_grad = [split(b * dot3(d, u)) for b, d, u in zip(beta, inverse, update_grad)]
    for j in heads:
        high = jnp.concatenate([-value_grad[j][0], out_grad[j]], axis=0)
        start = jnp.broadcast_to(rows[j]["start"], (8, head_dim)).T[:, :1]
        state_grad = start * (
            dot(across[j][0], high)
            + dot(across[j][1], high)
            - dot(across[j][0][:, :tokens], value_grad[j][1])
        )
        coded_ref[:, j] = encode(state_grad).reshape(pieces, head_dim // pieces, head_dim)
        value_grad_ref[0, :, lanes[j]] = value_grad[j][0]
        value_low_ref[0, :, lanes[j]] = value_grad[j][1]
        inverse_ref[0, j] = jnp.concatenate(inverse[j], axis=1)


def choose_kernel(prompt_ref, state_ref, *rest):
    chosen, (held_ref, arrival, departure) = rest[:-3], rest[-3:]
    members, count = len(chosen), chosen[0].shape[0]
    group_first = lax.axis_index("grp") * members * count
    reads, writes = [], []
    for step in range(members):
        receiver, _ = meeting(step)
        for b in range(count):
            prompt = prompt_ref[group_first + receiver * count + b]
            slot = step * count + b
            reads.append(
                pltpu.make_async_copy(state_ref.at[prompt], held_ref.at[slot], arrival.at[slot])
            )
            writes.append(
                pltpu.make_async_copy(held_ref.at[slot], chosen[step].at[b], departure.at[slot])
            )
    for read in reads:
        read.start()
    for read, write in zip(reads, writes):
        read.wait()
        write.start()
    for write in writes:
        write.wait()


def second_kernel(
    per_step,
    members,
    valid_ref,
    query_ref,
    key_ref,
    value_ref,
    decay_ref,
    grad_ref,
    beta_ref,
    value_grad_ref,
    value_low_ref,
    inverse_ref,
    *rest,
):
    arrived, rest = rest[:members], rest[members:]
    query_grad_ref, key_grad_ref, decay_grad_ref, beta_grad_ref, strength_ref = rest[:5]
    state_ref, arrival = rest[5:]
    tokens = query_ref.shape[1]
    head_dim = query_ref.shape[2] // per_step
    step = pl.program_id(1)

    @pl.when(step == 0)
    def _():
        copies = []
        for i in range(members):
            _, sender = meeting(i)
            copies.append(
                pltpu.make_async_copy(
                    arrived[i].at[pl.program_id(0)], state_ref.at[sender], arrival.at[i]
                )
            )
        for copy in copies:
            copy.start()
        for copy in copies:
            copy.wait()
        strength_ref[...] = jnp.zeros_like(strength_ref)

    valid = valid_ref[own_branch(pl.num_programs(0)) + pl.program_id(0)]
    row, col = iota2((tokens, tokens), 0), iota2((tokens, tokens), 1)
    tri = (row >= col).astype(BF16)
    later = (row <= col).astype(BF16)
    later = jnp.concatenate([later, later], axis=1)
    keep = iota2((tokens, 1), 0) < valid
    logits = beta_ref[0].astype(F32).T
    betas = jax.nn.sigmoid(logits) * keep.astype(F32)
    heads = range(per_step)
    lanes = [slice(j * head_dim, (j + 1) * head_dim) for j in heads]
    number = [step * per_step + j for j in heads]
    here = state_ref.shape[1]
    rows = [
        decayed_rows(
            query_ref[0, :, lanes[j]],
            key_ref[0, :, lanes[j]],
            decay_ref[0, :, lanes[j]],
            valid,
            tri,
        )
        for j in heads
    ]
    beta = [head_column(betas, n) for n in number]
    state = [state_ref[n // here, n % here] for n in number]
    target = [
        value_ref[0, :, lanes[j]].astype(F32)
        - dot3(split(rows[j]["key_forward"] * rows[j]["start"]), split(state[j]))
        for j in heads
    ]
    update = [
        split(
            dot3(
                split((b * x).T),
                (inverse_ref[0, j, :, :tokens], inverse_ref[0, j, :, tokens:]),
            )
        )
        for j, b, x in zip(heads, beta, target)
    ]
    against = [stack(u, split(x.T), 1) for u, x in zip(update, state)]
    products = []
    for j in heads:
        grad = grad_ref[0, :, lanes[j]]
        grad = jnp.where(keep, grad, jnp.zeros_like(grad))
        high = jnp.concatenate([grad, -value_grad_ref[0, :, lanes[j]]], axis=0)
        total = dot(high, against[j][0]) + dot(high, against[j][1])
        low = dot(value_low_ref[0, :, lanes[j]], against[j][0])
        products.append((total[:tokens], total[tokens:] - low))

    strengths = strength_ref[...]
    attend_grad = [jnp.where(row >= col, p[0][:, :tokens], 0.0) for p in products]
    coupling_grad = [jnp.where(row > col, p[1][:, :tokens], 0.0) for p in products]
    through_rows = [
        dot3(split(jnp.concatenate([p, c], axis=0)), split(r["key_earlier"]))
        for p, c, r in zip(attend_grad, coupling_grad, rows)
    ]
    earlier = [
        dot3(
            split(jnp.concatenate([p.T, c.T], axis=1)),
            split(jnp.concatenate([r["query_forward"], r["key_forward"]], axis=0)),
        )
        for p, c, r in zip(attend_grad, coupling_grad, rows)
    ]
    for j in heads:
        r = rows[j]
        query_forward = products[j][0][:, tokens:] * r["start"] + through_rows[j][:tokens]
        key_forward = products[j][1][:, tokens:] * r["start"] + through_rows[j][tokens:]
        query_unit_grad = query_forward * (r["grow"] * head_dim**-0.5)
        key_later = key_forward * r["grow"]
        key_before = earlier[j] * r["shrink"]
        key_unit_grad = key_later + key_before
        decay_step = r["unit_query"] * query_unit_grad + r["unit_key"] * (key_later - key_before)
        decay_grad = dot(later, jnp.concatenate(split(decay_step), axis=0))
        decay_grad_ref[0, :, lanes[j]] = jnp.where(keep, decay_grad, 0.0).astype(BF16)
        along = jnp.sum(r["unit_query"] * query_unit_grad, axis=1, keepdims=True)
        query_grad_ref[0, :, lanes[j]] = (
            r["query_scale"] * (query_unit_grad - r["unit_query"] * along)
        ).astype(BF16)
        along = jnp.sum(r["unit_key"] * key_unit_grad, axis=1, keepdims=True)
        key_grad_ref[0, :, lanes[j]] = (
            r["key_scale"] * (key_unit_grad - r["unit_key"] * along)
        ).astype(BF16)
        strength = jnp.sum(
            jnp.where(row == col, -products[j][1][:, :tokens], 0.0), axis=1, keepdims=True
        )
        strengths = jnp.where(iota2(logits.shape, 1) == number[j], strength, strengths)
    strength_ref[...] = strengths

    @pl.when(step == pl.num_programs(1) - 1)
    def _():
        beta_grad_ref[0] = (strength_ref[...] * jnp.exp(-logits)).T.astype(BF16)


def sum_kernel(prompt_ref, coded_ref, out_ref, total_ref):
    total_ref[...] = jnp.zeros_like(total_ref)

    def add(branch, carry):
        total_ref[prompt_ref[branch]] += decode(coded_ref[branch])
        return carry

    lax.fori_loop(0, coded_ref.shape[0], add, 0, unroll=4)
    out_ref[...] = encode(total_ref[...])


def spread_kernel(*refs):
    out_ref = refs[-1]
    pieces = refs[:-1]
    chips = len(pieces) // 2
    for i, piece in enumerate(pieces):
        place = source(i % chips, chips) ^ (i // chips)
        out_ref[:, :, pl.ds(place, 1)] = decode(piece[...])[:, :, None]


def source(step, chips):
    me = lax.axis_index("grp")
    if chips & (chips - 1) == 0:
        return me ^ (2 * step)
    return (me // 2 - step + chips) % chips * 2 + me % 2


def gather_pieces(piece, beside):
    size = lax.axis_size("grp")
    chips = size // 2
    power = chips & (chips - 1) == 0
    pieces = [piece]
    for step in range(1, chips):
        other = [((c ^ step) if power else (c + step) % chips) for c in range(chips)]
        moves = [(2 * c + core, 2 * other[c] + core) for c in range(chips) for core in range(2)]
        pieces.append(lax.ppermute(piece, "grp", moves))
    pieces, _ = lax.optimization_barrier((pieces, beside))
    swap = [(i, i ^ 1) for i in range(size)]
    return pieces + [lax.ppermute(x, "grp", swap) for x in pieces]


def moves_at(step, members):
    if members & (members - 1) == 0:
        return [(m, m ^ step) for m in range(members)]
    return [(m, (m + step) % members) for m in range(members)]


def meeting(step):
    members = lax.axis_size("head")
    me = lax.axis_index("head")
    if members & (members - 1) == 0:
        return me ^ step, me ^ step
    return (me + step) % members, (me - step + members) % members


def per_device(
    query_rows,
    key_rows,
    value_rows,
    log_decay,
    beta_logit,
    out_grad,
    fork_state,
    branch_prompt,
    valid_len,
):
    count, tokens, width = query_rows.shape
    prompts, heads_here, head_dim, _ = fork_state.shape
    members = lax.axis_size("head")
    groups = lax.axis_size("grp")
    heads = members * heads_here
    piece_rows = head_dim // groups
    per_step = next(n for n in (8, 4, 2, 1) if heads % n == 0)
    steps = heads // per_step
    params = pltpu.CompilerParams(vmem_limit_bytes=60 * 2**20)
    rows_type = jax.ShapeDtypeStruct(query_rows.shape, BF16)
    units = count * heads * tokens * tokens * head_dim
    betas = jnp.swapaxes(beta_logit, 1, 2)
    anywhere = pl.BlockSpec(memory_space=pl.ANY)

    row_block = pl.BlockSpec((1, tokens, per_step * head_dim), lambda b, i, *_: (b, 0, i))
    beta_block = pl.BlockSpec((1, heads, tokens), lambda b, i, *_: (b, 0, 0))
    inverse_block = pl.BlockSpec(
        (1, per_step, tokens, 2 * tokens), lambda b, i, *_: (b, i, 0, 0)
    )
    value_grad, value_low, inverse, coded = pl.pallas_call(
        functools.partial(first_kernel, per_step, 16),
        grid_spec=pltpu.PrefetchScalarGridSpec(
            num_scalar_prefetch=1,
            grid=(count, steps),
            in_specs=[row_block] * 4 + [beta_block],
            out_specs=[
                row_block,
                row_block,
                inverse_block,
                pl.BlockSpec(
                    (groups, per_step, piece_rows, head_dim),
                    lambda b, i, *_: (0, b * steps + i, 0, 0),
                ),
            ],
        ),
        out_shape=[
            rows_type,
            rows_type,
            jax.ShapeDtypeStruct((count, heads, tokens, 2 * tokens), BF16),
            jax.ShapeDtypeStruct((groups, count * heads, piece_rows, head_dim), BF16),
        ],
        compiler_params=params,
        cost_estimate=pl.CostEstimate(flops=100 * units, bytes_accessed=2**23, transcendentals=0),
        name="state_independent",
    )(valid_len, query_rows, key_rows, log_decay, out_grad, betas)

    states_after, coded = lax.optimization_barrier((fork_state, coded))
    states = pl.pallas_call(
        choose_kernel,
        grid_spec=pltpu.PrefetchScalarGridSpec(
            num_scalar_prefetch=1,
            grid=(1,),
            in_specs=[anywhere],
            out_specs=[anywhere] * members,
            scratch_shapes=[
                pltpu.VMEM((members * count, heads_here, head_dim, head_dim), F32),
                pltpu.SemaphoreType.DMA((members * count,)),
                pltpu.SemaphoreType.DMA((members * count,)),
            ],
        ),
        out_shape=[jax.ShapeDtypeStruct((count, heads_here, head_dim, head_dim), F32)] * members,
        compiler_params=params,
        name="choose_states",
    )(branch_prompt, states_after)
    states = [states[0]] + [
        lax.ppermute(states[step], "head", moves_at(step, members)) for step in range(1, members)
    ]

    coded = (
        coded.reshape(groups, count, members, heads_here, piece_rows, head_dim)
        .transpose(0, 2, 1, 3, 4, 5)
        .reshape(groups * members, count, heads_here, piece_rows, head_dim)
    )
    arrived = lax.all_to_all(coded, ("grp", "head"), 0, 0, tiled=True)

    query_grad, key_grad, decay_grad, beta_grad = pl.pallas_call(
        functools.partial(second_kernel, per_step, members),
        grid_spec=pltpu.PrefetchScalarGridSpec(
            num_scalar_prefetch=1,
            grid=(count, steps),
            in_specs=[row_block] * 5
            + [beta_block, row_block, row_block, inverse_block]
            + [anywhere] * members,
            out_specs=[row_block] * 3 + [beta_block],
            scratch_shapes=[
                pltpu.VMEM((tokens, heads), F32),
                pltpu.VMEM((members, heads_here, head_dim, head_dim), F32),
                pltpu.SemaphoreType.DMA((members,)),
            ],
        ),
        out_shape=[rows_type] * 3 + [jax.ShapeDtypeStruct((count, heads, tokens), BF16)],
        compiler_params=params,
        cost_estimate=pl.CostEstimate(flops=120 * units, bytes_accessed=2**23, transcendentals=0),
        name="state_dependent",
    )(
        valid_len,
        query_rows,
        key_rows,
        value_rows,
        log_decay,
        out_grad,
        betas,
        value_grad,
        value_low,
        inverse,
        *states,
    )

    piece_shape = (prompts, heads_here, piece_rows, head_dim)
    branches = groups * members * count
    whole = pl.BlockSpec(memory_space=pltpu.VMEM)
    scalars = pl.BlockSpec(memory_space=pltpu.SMEM)
    piece = pl.pallas_call(
        sum_kernel,
        in_specs=[scalars, whole],
        out_specs=whole,
        out_shape=jax.ShapeDtypeStruct(piece_shape, BF16),
        scratch_shapes=[pltpu.VMEM(piece_shape, F32)],
        compiler_params=params,
        name="sum_by_prompt",
    )(branch_prompt, arrived.reshape(branches, heads_here, piece_rows, head_dim))
    pieces = gather_pieces(piece, query_grad)
    grad_fork = pl.pallas_call(
        spread_kernel,
        in_specs=[whole] * len(pieces),
        out_specs=whole,
        out_shape=jax.ShapeDtypeStruct(
            (prompts, heads_here, groups, piece_rows, head_dim), F32
        ),
        compiler_params=params,
        name="spread_pieces",
    )(*pieces)
    return (
        query_grad,
        key_grad,
        value_grad,
        decay_grad,
        jnp.swapaxes(beta_grad, 1, 2),
        grad_fork.reshape(fork_state.shape),
    )


def solution(mesh):
    rows = P(("grp", "head"), None, None)
    state = P(None, "head", None, None)
    return jax.shard_map(
        per_device,
        mesh=mesh,
        in_specs=(rows, rows, rows, rows, rows, rows, state, P(), P()),
        out_specs=(rows, rows, rows, rows, rows, state),
        check_vma=False,
    )
```

```python
import functools

import jax
import jax.numpy as jnp
from jax import lax
from jax.experimental import pallas as pl
from jax.experimental.pallas import tpu as pltpu
from jax.sharding import PartitionSpec as P

HIGH = lax.Precision.HIGH
NN = ((1,), (0,))
NT = ((1,), (1,))
TN = ((0,), (0,))
F32 = jnp.float32
BF16 = jnp.bfloat16


def dot(a, b, dims=NN, precision=None):
    return lax.dot_general(
        a, b, (dims, ((), ())), preferred_element_type=F32, precision=precision
    )


def split(x):
    high = x.astype(BF16)
    return high, (x - high.astype(F32)).astype(BF16)


def encode(x):
    return (x * x * x * jnp.abs(x)).astype(BF16)


def decode(y):
    wide = y.astype(F32)
    root = lax.rsqrt(lax.rsqrt(jnp.abs(wide)))
    return jnp.where(wide < 0, -root, root)


def iota2(shape, axis):
    return lax.broadcasted_iota(jnp.int32, shape, axis)


def dot3(a, b):
    return dot(a[0], b[0]) + dot(a[1], b[0]) + dot(a[0], b[1])


def stack(a, b, axis):
    return tuple(jnp.concatenate([x, y], axis=axis) for x, y in zip(a, b))


def unit_upper_inverse(matrices, width):
    size = matrices[0].shape[0]
    blocks = size // width
    row, col = iota2((size, size), 0), iota2((size, size), 1)
    on_block = row // width == col // width
    lane = iota2((8, size), 1)
    identity = (iota2((width, size), 0) == iota2((width, size), 1) % width).astype(F32)
    inverses = []
    for a in matrices:
        compact = jnp.sum(jnp.where(on_block, a, 0.0).reshape(blocks, width, size), axis=0)
        slabs = [compact[i : i + 8] for i in range(0, width, 8)]
        result = [identity[i : i + 8] for i in range(0, width, 8)]
        for m in reversed(range(1, width)):
            source = result[m // 8][m % 8 : m % 8 + 1]
            for i in range((m - 1) // 8 + 1):
                column = jnp.take_along_axis(slabs[i], lane // width * width + m, axis=1)
                result[i] = result[i] - column * source
        inverses.append(jnp.where(on_block, jnp.concatenate(result * blocks, axis=0), 0.0))
    while width * 2 < size:
        upper = (row // (2 * width) == col // (2 * width)) & (row // width < col // width)
        parts = [split(d) for d in inverses]
        inner = [dot3(split(jnp.where(upper, a, 0.0)), d) for a, d in zip(matrices, parts)]
        inverses = [d - dot3(p, split(x)) for d, p, x in zip(inverses, parts, inner)]
        width *= 2
    results = []
    first = [split(d[:width, :width]) for d in inverses]
    second = [split(d[width:, width:]) for d in inverses]
    inner = [dot3(split(a[:width, width:]), d) for a, d in zip(matrices, second)]
    corner = [dot3(d, split(x)) for d, x in zip(first, inner)]
    for d, x in zip(inverses, corner):
        top = jnp.concatenate([d[:width, :width], -x], axis=1)
        results.append(jnp.concatenate([top, d[width:]], axis=0))
    return results


def decayed_rows(query_in, key_in, decay_in, valid, tri):
    tokens, head_dim = query_in.shape
    row = iota2((tokens, 1), 0)
    query = query_in.astype(F32)
    key = key_in.astype(F32)
    query_scale = lax.rsqrt(jnp.sum(query * query, axis=1, keepdims=True) + 1e-06)
    key_scale = lax.rsqrt(jnp.sum(key * key, axis=1, keepdims=True) + 1e-06)
    unit_query = query * query_scale
    unit_key = key * key_scale
    decay = jnp.where(row < valid, decay_in, jnp.zeros_like(decay_in))
    cumulative = dot(tri, decay)
    middle = cumulative[tokens // 2 - 1 : tokens // 2]
    cumulative = cumulative - middle
    grow = jnp.exp(cumulative)
    shrink = jnp.exp(-cumulative)
    return dict(
        unit_query=unit_query,
        unit_key=unit_key,
        query_scale=query_scale,
        key_scale=key_scale,
        grow=grow,
        shrink=shrink,
        start=jnp.exp(middle),
        key_forward=unit_key * grow,
        key_earlier=unit_key * shrink,
        query_forward=unit_query * (grow * head_dim**-0.5),
    )


def own_branch(count):
    place = lax.axis_index("grp") * lax.axis_size("head") + lax.axis_index("head")
    return place * count


def halves(heads, head_dim):
    parts = 2 if heads % 2 == 0 else 1
    size = heads // parts
    numbers = [range(p * size, (p + 1) * size) for p in range(parts)]
    return [(list(n), slice(n[0] * head_dim, (n[-1] + 1) * head_dim)) for n in numbers]


def start_all(pairs, done, first=0):
    copies = [pltpu.make_async_copy(a, b, done.at[first + i]) for i, (a, b) in enumerate(pairs)]
    for copy in copies:
        copy.start()
    return copies


def head_lanes(j, head_dim):
    return slice(j * head_dim, (j + 1) * head_dim)


def first_kernel(
    width,
    valid_ref,
    query_hbm,
    key_hbm,
    decay_hbm,
    grad_hbm,
    beta_hbm,
    value_grad_hbm,
    value_low_hbm,
    inverse_hbm,
    coded_hbm,
    rows_ref,
    beta_ref,
    value_grad_ref,
    value_low_ref,
    inverse_ref,
    coded_ref,
    arrival,
    departure,
):
    branch = pl.program_id(0)
    heads, tokens, _ = inverse_ref.shape
    pieces, _, piece_rows, head_dim = coded_ref.shape
    parts = halves(heads, head_dim)
    inputs = (query_hbm, key_hbm, decay_hbm)

    def fetch(p):
        lanes = parts[p][1]
        return start_all(
            [(x.at[branch, :, lanes], rows_ref.at[i, :, lanes]) for i, x in enumerate(inputs)],
            arrival,
            3 * p,
        )

    arriving = fetch(0)
    valid = valid_ref[own_branch(pl.num_programs(0)) + branch]
    row, col = iota2((tokens, tokens), 0), iota2((tokens, tokens), 1)
    tri = (row >= col).astype(BF16)
    keep = iota2((tokens, 1), 0) < valid
    lane_keep = iota2((1, tokens), 1) < valid
    rows, across, scores = [], [], []
    for p, (numbers, _) in enumerate(parts):
        for copy in arriving:
            copy.wait()
        if p + 1 < len(parts):
            arriving = fetch(p + 1)
        else:
            arriving = start_all(
                [(beta_hbm.at[branch], beta_ref), (grad_hbm.at[branch], rows_ref.at[3])],
                arrival,
                3 * len(parts),
            )
        fresh = [
            decayed_rows(*(rows_ref[i, :, head_lanes(j, head_dim)] for i in range(3)), valid, tri)
            for j in numbers
        ]
        turned = [
            split(jnp.concatenate([r["key_forward"], r["query_forward"]], axis=0).T) for r in fresh
        ]
        scores += [dot3(split(r["key_earlier"]), x) for r, x in zip(fresh, turned)]
        rows += fresh
        across += turned
    for copy in arriving:
        copy.wait()
    out_grad = []
    for j in range(heads):
        grad = rows_ref[3, :, head_lanes(j, head_dim)]
        out_grad.append(jnp.where(keep, grad, jnp.zeros_like(grad)))
    flat_betas = jax.nn.sigmoid(beta_ref[...].astype(F32)) * lane_keep.astype(F32)
    betas = flat_betas.T
    every = range(heads)
    beta = [betas[:, j : j + 1] for j in every]
    coupling = [
        jnp.where(row < col, s[:, :tokens] * flat_betas[j : j + 1], 0.0)
        for j, s in enumerate(scores)
    ]
    attend = [split(jnp.where(row <= col, s[:, tokens:], 0.0)) for s in scores]
    inverse = [split(x) for x in unit_upper_inverse(coupling, width)]
    for j in every:
        inverse_ref[j] = jnp.concatenate(inverse[j], axis=1)
    leaving = start_all([(inverse_ref, inverse_hbm.at[branch])], departure)
    update_grad = [split(dot(p[0], g) + dot(p[1], g)) for p, g in zip(attend, out_grad)]
    value_grad = [split(b * dot3(d, u)) for b, d, u in zip(beta, inverse, update_grad)]
    for j in every:
        value_grad_ref[:, head_lanes(j, head_dim)] = value_grad[j][0]
        value_low_ref[:, head_lanes(j, head_dim)] = value_grad[j][1]
    leaving += start_all(
        [
            (value_grad_ref, value_grad_hbm.at[branch]),
            (value_low_ref, value_low_hbm.at[branch]),
        ],
        departure,
        1,
    )
    for p, (numbers, _) in enumerate(parts):
        for j in numbers:
            high = jnp.concatenate([-value_grad[j][0], out_grad[j]], axis=0)
            start = jnp.broadcast_to(rows[j]["start"], (8, head_dim)).T[:, :1]
            state_grad = start * (
                dot(across[j][0], high)
                + dot(across[j][1], high)
                - dot(across[j][0][:, :tokens], value_grad[j][1])
            )
            coded_ref[:, j] = encode(state_grad).reshape(pieces, piece_rows, head_dim)
        first, size = numbers[0], len(numbers)
        copy = pltpu.make_async_copy(
            coded_ref.at[:, pl.ds(first, size)],
            coded_hbm.at[:, pl.ds(branch * heads + first, size)],
            departure.at[3 + p],
        )
        copy.start()
        leaving.append(copy)
    for copy in leaving:
        copy.wait()


def choose_kernel(prompt_ref, state_ref, *rest):
    chosen, (held_ref, arrival, departure) = rest[:-3], rest[-3:]
    members, count = len(chosen), chosen[0].shape[0]
    group_first = lax.axis_index("grp") * members * count
    reads, writes = [], []
    for step in range(members):
        receiver, _ = meeting(step)
        for b in range(count):
            prompt = prompt_ref[group_first + receiver * count + b]
            slot = step * count + b
            reads.append(
                pltpu.make_async_copy(state_ref.at[prompt], held_ref.at[slot], arrival.at[slot])
            )
            writes.append(
                pltpu.make_async_copy(held_ref.at[slot], chosen[step].at[b], departure.at[slot])
            )
    for read in reads:
        read.start()
    for read, write in zip(reads, writes):
        read.wait()
        write.start()
    for write in writes:
        write.wait()


def second_kernel(members, valid_ref, *refs):
    row_hbm, (beta_hbm, inverse_hbm), refs = refs[:7], refs[7:9], refs[9:]
    state_hbm, out_hbm, refs = refs[:members], refs[members : members + 4], refs[members + 4 :]
    rows_ref, beta_ref, inverse_ref, state_ref, out_ref, beta_grad_ref, arrival, departure = refs
    branch = pl.program_id(0)
    heads, tokens, _ = inverse_ref.shape
    head_dim = rows_ref.shape[2] // heads
    here = state_ref.shape[1]
    parts = halves(heads, head_dim)
    pairs = []
    for numbers, lanes in parts:
        for i, ref in enumerate(row_hbm):
            pairs.append((ref.at[branch, :, lanes], rows_ref.at[i, :, lanes]))
        some = pl.ds(numbers[0], len(numbers))
        pairs.append((inverse_hbm.at[branch, some], inverse_ref.at[some]))
    for i in range(members):
        _, sender = meeting(i)
        pairs.append((state_hbm[i].at[branch], state_ref.at[sender]))
    pairs.append((beta_hbm.at[branch], beta_ref))
    arriving = start_all(pairs, arrival)
    each = len(row_hbm) + 1

    valid = valid_ref[own_branch(pl.num_programs(0)) + branch]
    row, col = iota2((tokens, tokens), 0), iota2((tokens, tokens), 1)
    tri = (row >= col).astype(BF16)
    later = (row <= col).astype(BF16)
    later = jnp.concatenate([later, later], axis=1)
    keep = iota2((tokens, 1), 0) < valid
    rows, own_rows = [], []
    for p, (numbers, _) in enumerate(parts):
        for copy in arriving[each * p : each * (p + 1)]:
            copy.wait()
        for j in numbers:
            own_rows.append([rows_ref[i, :, head_lanes(j, head_dim)] for i in range(len(row_hbm))])
            query, key, _, decay = own_rows[j][:4]
            rows.append(decayed_rows(query, key, decay, valid, tri))
    for copy in arriving[each * len(parts) :]:
        copy.wait()
    logits = beta_ref[...].astype(F32).T
    betas = jax.nn.sigmoid(logits) * keep.astype(F32)
    every = range(heads)
    state = [state_ref[j // here, j % here] for j in every]
    target = [
        own_rows[j][2].astype(F32)
        - dot3(split(rows[j]["key_forward"] * rows[j]["start"]), split(state[j]))
        for j in every
    ]
    update = [
        split(
            dot3(
                split((betas[:, j : j + 1] * target[j]).T),
                (inverse_ref[j, :, :tokens], inverse_ref[j, :, tokens:]),
            )
        )
        for j in every
    ]
    against = [stack(u, split(x.T), 1) for u, x in zip(update, state)]
    products = []
    for j in every:
        grad, high, low = own_rows[j][4:]
        grad = jnp.where(keep, grad, jnp.zeros_like(grad))
        high = jnp.concatenate([grad, -high], axis=0)
        total = dot(high, against[j][0]) + dot(high, against[j][1])
        products.append((total[:tokens], total[tokens:] - dot(low, against[j][0])))
    attend_grad = [jnp.where(row >= col, p[0][:, :tokens], 0.0) for p in products]
    coupling_grad = [jnp.where(row > col, p[1][:, :tokens], 0.0) for p in products]
    through_rows = [
        dot3(split(jnp.concatenate([p, c], axis=0)), split(r["key_earlier"]))
        for p, c, r in zip(attend_grad, coupling_grad, rows)
    ]
    earlier = [
        dot3(
            split(jnp.concatenate([p.T, c.T], axis=1)),
            split(jnp.concatenate([r["query_forward"], r["key_forward"]], axis=0)),
        )
        for p, c, r in zip(attend_grad, coupling_grad, rows)
    ]
    strengths = jnp.zeros(logits.shape, F32)
    leaving = []
    for numbers, lanes in parts:
        for j in numbers:
            r = rows[j]
            query_forward = products[j][0][:, tokens:] * r["start"] + through_rows[j][:tokens]
            key_forward = products[j][1][:, tokens:] * r["start"] + through_rows[j][tokens:]
            query_unit_grad = query_forward * (r["grow"] * head_dim**-0.5)
            key_later = key_forward * r["grow"]
            key_before = earlier[j] * r["shrink"]
            key_unit_grad = key_later + key_before
            decay_step = r["unit_query"] * query_unit_grad + r["unit_key"] * (
                key_later - key_before
            )
            decay_grad = dot(later, jnp.concatenate(split(decay_step), axis=0))
            decay_grad = jnp.where(keep, decay_grad, 0.0)
            along = jnp.sum(r["unit_query"] * query_unit_grad, axis=1, keepdims=True)
            query_grad = r["query_scale"] * (query_unit_grad - r["unit_query"] * along)
            along = jnp.sum(r["unit_key"] * key_unit_grad, axis=1, keepdims=True)
            key_grad = r["key_scale"] * (key_unit_grad - r["unit_key"] * along)
            for i, grad in enumerate((query_grad, key_grad, decay_grad)):
                out_ref[i, :, head_lanes(j, head_dim)] = grad.astype(BF16)
            strength = jnp.sum(
                jnp.where(row == col, -products[j][1][:, :tokens], 0.0), axis=1, keepdims=True
            )
            strengths = jnp.where(iota2(logits.shape, 1) == j, strength, strengths)
        for i in range(3):
            copy = pltpu.make_async_copy(
                out_ref.at[i, :, lanes], out_hbm[i].at[branch, :, lanes], departure.at[len(leaving)]
            )
            copy.start()
            leaving.append(copy)
    beta_grad_ref[...] = (strengths * jnp.exp(-logits)).T.astype(BF16)
    copy = pltpu.make_async_copy(beta_grad_ref, out_hbm[3].at[branch], departure.at[len(leaving)])
    copy.start()
    leaving.append(copy)
    for copy in leaving:
        copy.wait()


def sum_kernel(prompt_ref, coded_ref, out_ref, total_ref):
    total_ref[...] = jnp.zeros_like(total_ref)

    def add(branch, carry):
        total_ref[prompt_ref[branch]] += decode(coded_ref[branch])
        return carry

    lax.fori_loop(0, coded_ref.shape[0], add, 0, unroll=8)
    out_ref[...] = encode(total_ref[...])


def spread_kernel(*refs):
    pieces, (out_hbm, out_ref, departure) = refs[:-3], refs[-3:]
    chips = len(pieces) // 2
    prompts = out_ref.shape[0]
    parts = next(n for n in (4, 2, 1) if prompts % n == 0)
    size = prompts // parts
    leaving = []
    for p in range(parts):
        some = pl.ds(p * size, size)
        for i, piece in enumerate(pieces):
            place = source(i % chips, chips) ^ (i // chips)
            out_ref[some, :, pl.ds(place, 1)] = decode(piece[some])[:, :, None]
        leaving.append(pltpu.make_async_copy(out_ref.at[some], out_hbm.at[some], departure.at[p]))
        leaving[p].start()
    for copy in leaving:
        copy.wait()


def source(step, chips):
    me = lax.axis_index("grp")
    if chips & (chips - 1) == 0:
        return me ^ (2 * step)
    return (me // 2 - step + chips) % chips * 2 + me % 2


def gather_pieces(piece, beside):
    size = lax.axis_size("grp")
    chips = size // 2
    power = chips & (chips - 1) == 0
    pieces = [piece]
    for step in range(1, chips):
        other = [((c ^ step) if power else (c + step) % chips) for c in range(chips)]
        moves = [(2 * c + core, 2 * other[c] + core) for c in range(chips) for core in range(2)]
        pieces.append(lax.ppermute(piece, "grp", moves))
    pieces, _ = lax.optimization_barrier((pieces, beside))
    swap = [(i, i ^ 1) for i in range(size)]
    return pieces + [lax.ppermute(x, "grp", swap) for x in pieces]


def moves_at(step, members):
    if members & (members - 1) == 0:
        return [(m, m ^ step) for m in range(members)]
    return [(m, (m + step) % members) for m in range(members)]


def meeting(step):
    members = lax.axis_size("head")
    me = lax.axis_index("head")
    if members & (members - 1) == 0:
        return me ^ step, me ^ step
    return (me + step) % members, (me - step + members) % members


def per_device(
    query_rows,
    key_rows,
    value_rows,
    log_decay,
    beta_logit,
    out_grad,
    fork_state,
    branch_prompt,
    valid_len,
):
    count, tokens, width = query_rows.shape
    prompts, heads_here, head_dim, _ = fork_state.shape
    members = lax.axis_size("head")
    groups = lax.axis_size("grp")
    heads = members * heads_here
    piece_rows = head_dim // groups
    params = pltpu.CompilerParams(vmem_limit_bytes=62 * 2**20)
    small = pltpu.CompilerParams(vmem_limit_bytes=16 * 2**20)
    rows_type = jax.ShapeDtypeStruct(query_rows.shape, BF16)
    units = count * heads * tokens * tokens * head_dim
    betas = jnp.swapaxes(beta_logit, 1, 2)
    anywhere = pl.BlockSpec(memory_space=pl.ANY)

    parts = len(halves(heads, head_dim))
    value_grad, value_low, inverse, coded = pl.pallas_call(
        functools.partial(first_kernel, 16),
        grid_spec=pltpu.PrefetchScalarGridSpec(
            num_scalar_prefetch=1,
            grid=(count,),
            in_specs=[anywhere] * 5,
            out_specs=[anywhere] * 4,
            scratch_shapes=[
                pltpu.VMEM((4, tokens, width), BF16),
                pltpu.VMEM((heads, tokens), BF16),
                pltpu.VMEM((tokens, width), BF16),
                pltpu.VMEM((tokens, width), BF16),
                pltpu.VMEM((heads, tokens, 2 * tokens), BF16),
                pltpu.VMEM((groups, heads, piece_rows, head_dim), BF16),
                pltpu.SemaphoreType.DMA((3 * parts + 2,)),
                pltpu.SemaphoreType.DMA((3 + parts,)),
            ],
        ),
        out_shape=[
            rows_type,
            rows_type,
            jax.ShapeDtypeStruct((count, heads, tokens, 2 * tokens), BF16),
            jax.ShapeDtypeStruct((groups, count * heads, piece_rows, head_dim), BF16),
        ],
        compiler_params=params,
        cost_estimate=pl.CostEstimate(flops=100 * units, bytes_accessed=2**23, transcendentals=0),
        name="state_independent",
    )(valid_len, query_rows, key_rows, log_decay, out_grad, betas)

    states_after, coded = lax.optimization_barrier((fork_state, coded))
    states = pl.pallas_call(
        choose_kernel,
        grid_spec=pltpu.PrefetchScalarGridSpec(
            num_scalar_prefetch=1,
            grid=(1,),
            in_specs=[anywhere],
            out_specs=[anywhere] * members,
            scratch_shapes=[
                pltpu.VMEM((members * count, heads_here, head_dim, head_dim), F32),
                pltpu.SemaphoreType.DMA((members * count,)),
                pltpu.SemaphoreType.DMA((members * count,)),
            ],
        ),
        out_shape=[jax.ShapeDtypeStruct((count, heads_here, head_dim, head_dim), F32)] * members,
        compiler_params=params,
        name="choose_states",
    )(branch_prompt, states_after)
    states = [states[0]] + [
        lax.ppermute(states[step], "head", moves_at(step, members)) for step in range(1, members)
    ]

    coded = (
        coded.reshape(groups, count, members, heads_here, piece_rows, head_dim)
        .transpose(0, 2, 1, 3, 4, 5)
        .reshape(groups * members, count, heads_here, piece_rows, head_dim)
    )
    arrived = lax.all_to_all(coded, ("grp", "head"), 0, 0, tiled=True)

    query_grad, key_grad, decay_grad, beta_grad = pl.pallas_call(
        functools.partial(second_kernel, members),
        grid_spec=pltpu.PrefetchScalarGridSpec(
            num_scalar_prefetch=1,
            grid=(count,),
            in_specs=[anywhere] * (9 + members),
            out_specs=[anywhere] * 4,
            scratch_shapes=[
                pltpu.VMEM((7, tokens, width), BF16),
                pltpu.VMEM((heads, tokens), BF16),
                pltpu.VMEM((heads, tokens, 2 * tokens), BF16),
                pltpu.VMEM((members, heads_here, head_dim, head_dim), F32),
                pltpu.VMEM((3, tokens, width), BF16),
                pltpu.VMEM((heads, tokens), BF16),
                pltpu.SemaphoreType.DMA((8 * parts + members + 1,)),
                pltpu.SemaphoreType.DMA((3 * parts + 1,)),
            ],
        ),
        out_shape=[rows_type] * 3 + [jax.ShapeDtypeStruct((count, heads, tokens), BF16)],
        compiler_params=params,
        cost_estimate=pl.CostEstimate(flops=120 * units, bytes_accessed=2**23, transcendentals=0),
        name="state_dependent",
    )(
        valid_len,
        query_rows,
        key_rows,
        value_rows,
        log_decay,
        out_grad,
        value_grad,
        value_low,
        betas,
        inverse,
        *states,
    )

    piece_shape = (prompts, heads_here, piece_rows, head_dim)
    branches = groups * members * count
    whole = pl.BlockSpec(memory_space=pltpu.VMEM)
    scalars = pl.BlockSpec(memory_space=pltpu.SMEM)
    piece = pl.pallas_call(
        sum_kernel,
        in_specs=[scalars, whole],
        out_specs=whole,
        out_shape=jax.ShapeDtypeStruct(piece_shape, BF16),
        scratch_shapes=[pltpu.VMEM(piece_shape, F32)],
        compiler_params=small,
        name="sum_by_prompt",
    )(branch_prompt, arrived.reshape(branches, heads_here, piece_rows, head_dim))
    pieces = gather_pieces(piece, query_grad)
    fork_shape = (prompts, heads_here, groups, piece_rows, head_dim)
    grad_fork = pl.pallas_call(
        spread_kernel,
        in_specs=[whole] * len(pieces),
        out_specs=anywhere,
        out_shape=jax.ShapeDtypeStruct(fork_shape, F32),
        scratch_shapes=[pltpu.VMEM(fork_shape, F32), pltpu.SemaphoreType.DMA((4,))],
        compiler_params=small,
        name="spread_pieces",
    )(*pieces)
    return (
        query_grad,
        key_grad,
        value_grad,
        decay_grad,
        jnp.swapaxes(beta_grad, 1, 2),
        grad_fork.reshape(fork_state.shape),
    )


def solution(mesh):
    rows = P(("grp", "head"), None, None)
    state = P(None, "head", None, None)
    return jax.shard_map(
        per_device,
        mesh=mesh,
        in_specs=(rows, rows, rows, rows, rows, rows, state, P(), P()),
        out_specs=(rows, rows, rows, rows, rows, state),
        check_vma=False,
    )
```

```python
import functools

import jax
import jax.numpy as jnp
from jax import lax
from jax.experimental import pallas as pl
from jax.experimental.pallas import tpu as pltpu
from jax.sharding import PartitionSpec as P

HIGH = lax.Precision.HIGH
NN = ((1,), (0,))
NT = ((1,), (1,))
TN = ((0,), (0,))
F32 = jnp.float32
BF16 = jnp.bfloat16


def dot(a, b, dims=NN, precision=None):
    return lax.dot_general(
        a, b, (dims, ((), ())), preferred_element_type=F32, precision=precision
    )


def split(x):
    high = x.astype(BF16)
    return high, (x - high.astype(F32)).astype(BF16)


def encode(x):
    return (x * x * x * jnp.abs(x)).astype(BF16)


def decode(y):
    wide = y.astype(F32)
    root = lax.rsqrt(lax.rsqrt(jnp.abs(wide)))
    return jnp.where(wide < 0, -root, root)


def iota2(shape, axis):
    return lax.broadcasted_iota(jnp.int32, shape, axis)


def dot3(a, b, dims=NN):
    return dot(a[0], b[0], dims) + dot(a[1], b[0], dims) + dot(a[0], b[1], dims)


def stack(a, b, axis):
    return tuple(jnp.concatenate([x, y], axis=axis) for x, y in zip(a, b))


def unit_upper_inverse(matrices, width):
    size = matrices[0].shape[0]
    blocks = size // width
    row, col = iota2((size, size), 0), iota2((size, size), 1)
    on_block = row // width == col // width
    lane = iota2((8, size), 1)
    identity = (iota2((width, size), 0) == iota2((width, size), 1) % width).astype(F32)
    inverses = []
    for a in matrices:
        compact = jnp.sum(jnp.where(on_block, a, 0.0).reshape(blocks, width, size), axis=0)
        slabs = [compact[i : i + 8] for i in range(0, width, 8)]
        result = [identity[i : i + 8] for i in range(0, width, 8)]
        for m in reversed(range(1, width)):
            source = result[m // 8][m % 8 : m % 8 + 1]
            for i in range((m - 1) // 8 + 1):
                column = jnp.take_along_axis(slabs[i], lane // width * width + m, axis=1)
                result[i] = result[i] - column * source
        inverses.append(jnp.where(on_block, jnp.concatenate(result * blocks, axis=0), 0.0))
    while width * 2 < size:
        upper = (row // (2 * width) == col // (2 * width)) & (row // width < col // width)
        parts = [split(d) for d in inverses]
        inner = [dot3(split(jnp.where(upper, a, 0.0)), d) for a, d in zip(matrices, parts)]
        inverses = [d - dot3(p, split(x)) for d, p, x in zip(inverses, parts, inner)]
        width *= 2
    results = []
    first = [split(d[:width, :width]) for d in inverses]
    second = [split(d[width:, width:]) for d in inverses]
    inner = [dot3(split(a[:width, width:]), d) for a, d in zip(matrices, second)]
    corner = [dot3(d, split(x)) for d, x in zip(first, inner)]
    for d, x in zip(inverses, corner):
        top = jnp.concatenate([d[:width, :width], -x], axis=1)
        results.append(jnp.concatenate([top, d[width:]], axis=0))
    return results


def decayed_rows(query_in, key_in, decay_in, valid, tri):
    tokens, head_dim = query_in.shape
    row = iota2((tokens, 1), 0)
    query = query_in.astype(F32)
    key = key_in.astype(F32)
    query_scale = lax.rsqrt(jnp.sum(query * query, axis=1, keepdims=True) + 1e-06)
    key_scale = lax.rsqrt(jnp.sum(key * key, axis=1, keepdims=True) + 1e-06)
    unit_query = query * query_scale
    unit_key = key * key_scale
    decay = jnp.where(row < valid, decay_in, jnp.zeros_like(decay_in))
    cumulative = dot(tri, decay)
    middle = cumulative[tokens // 2 - 1 : tokens // 2]
    cumulative = cumulative - middle
    grow = jnp.exp(cumulative)
    shrink = jnp.exp(-cumulative)
    return dict(
        unit_query=unit_query,
        unit_key=unit_key,
        query_scale=query_scale,
        key_scale=key_scale,
        grow=grow,
        shrink=shrink,
        start=jnp.exp(middle),
        key_forward=unit_key * grow,
        key_earlier=unit_key * shrink,
        query_forward=unit_query * (grow * head_dim**-0.5),
    )


def own_branch(count):
    place = lax.axis_index("grp") * lax.axis_size("head") + lax.axis_index("head")
    return place * count


def halves(heads, head_dim):
    parts = 2 if heads % 2 == 0 else 1
    size = heads // parts
    numbers = [range(p * size, (p + 1) * size) for p in range(parts)]
    return [(list(n), slice(n[0] * head_dim, (n[-1] + 1) * head_dim)) for n in numbers]


def start_all(pairs, done, first=0):
    copies = [pltpu.make_async_copy(a, b, done.at[first + i]) for i, (a, b) in enumerate(pairs)]
    for copy in copies:
        copy.start()
    return copies


def head_lanes(j, head_dim):
    return slice(j * head_dim, (j + 1) * head_dim)


def first_kernel(
    width,
    valid_ref,
    query_hbm,
    key_hbm,
    decay_hbm,
    grad_hbm,
    beta_hbm,
    value_grad_hbm,
    value_low_hbm,
    inverse_hbm,
    coded_hbm,
    rows_ref,
    beta_ref,
    value_grad_ref,
    value_low_ref,
    inverse_ref,
    coded_ref,
    arrival,
    departure,
):
    branch = pl.program_id(0)
    heads, tokens, _ = inverse_ref.shape
    pieces, _, piece_rows, head_dim = coded_ref.shape
    parts = halves(heads, head_dim)
    inputs = (query_hbm, key_hbm, decay_hbm)

    def fetch(p):
        lanes = parts[p][1]
        return start_all(
            [(x.at[branch, :, lanes], rows_ref.at[i, :, lanes]) for i, x in enumerate(inputs)],
            arrival,
            3 * p,
        )

    arriving = fetch(0)
    valid = valid_ref[own_branch(pl.num_programs(0)) + branch]
    row, col = iota2((tokens, tokens), 0), iota2((tokens, tokens), 1)
    tri = (row >= col).astype(BF16)
    keep = iota2((tokens, 1), 0) < valid
    lane_keep = iota2((1, tokens), 1) < valid
    rows, across, scores = [], [], []
    for p, (numbers, _) in enumerate(parts):
        for copy in arriving:
            copy.wait()
        if p + 1 < len(parts):
            arriving = fetch(p + 1)
        else:
            arriving = start_all(
                [(beta_hbm.at[branch], beta_ref), (grad_hbm.at[branch], rows_ref.at[3])],
                arrival,
                3 * len(parts),
            )
        fresh = [
            decayed_rows(*(rows_ref[i, :, head_lanes(j, head_dim)] for i in range(3)), valid, tri)
            for j in numbers
        ]
        turned = [
            split(jnp.concatenate([r["key_forward"], r["query_forward"]], axis=0).T) for r in fresh
        ]
        scores += [dot3(split(r["key_earlier"]), x) for r, x in zip(fresh, turned)]
        rows += fresh
        across += turned
    for copy in arriving:
        copy.wait()
    out_grad = []
    for j in range(heads):
        grad = rows_ref[3, :, head_lanes(j, head_dim)]
        out_grad.append(jnp.where(keep, grad, jnp.zeros_like(grad)))
    flat_betas = jax.nn.sigmoid(beta_ref[...].astype(F32)) * lane_keep.astype(F32)
    betas = flat_betas.T
    every = range(heads)
    beta = [betas[:, j : j + 1] for j in every]
    coupling = [
        jnp.where(row < col, s[:, :tokens] * flat_betas[j : j + 1], 0.0)
        for j, s in enumerate(scores)
    ]
    attend = [split(jnp.where(row <= col, s[:, tokens:], 0.0)) for s in scores]
    inverse = [split(x) for x in unit_upper_inverse(coupling, width)]
    for j in every:
        inverse_ref[j] = jnp.concatenate(inverse[j], axis=1)
    leaving = start_all([(inverse_ref, inverse_hbm.at[branch])], departure)
    update_grad = [split(dot(p[0], g) + dot(p[1], g)) for p, g in zip(attend, out_grad)]
    value_grad = [split(b * dot3(d, u)) for b, d, u in zip(beta, inverse, update_grad)]
    for j in every:
        value_grad_ref[:, head_lanes(j, head_dim)] = value_grad[j][0]
        value_low_ref[:, head_lanes(j, head_dim)] = value_grad[j][1]
    leaving += start_all(
        [
            (value_grad_ref, value_grad_hbm.at[branch]),
            (value_low_ref, value_low_hbm.at[branch]),
        ],
        departure,
        1,
    )
    for p, (numbers, _) in enumerate(parts):
        for j in numbers:
            high = jnp.concatenate([-value_grad[j][0], out_grad[j]], axis=0)
            start = jnp.broadcast_to(rows[j]["start"], (8, head_dim)).T[:, :1]
            state_grad = start * (
                dot(across[j][0], high)
                + dot(across[j][1], high)
                - dot(across[j][0][:, :tokens], value_grad[j][1])
            )
            coded_ref[:, j] = encode(state_grad).reshape(pieces, piece_rows, head_dim)
        first, size = numbers[0], len(numbers)
        copy = pltpu.make_async_copy(
            coded_ref.at[:, pl.ds(first, size)],
            coded_hbm.at[:, pl.ds(branch * heads + first, size)],
            departure.at[3 + p],
        )
        copy.start()
        leaving.append(copy)
    for copy in leaving:
        copy.wait()


def choose_kernel(prompt_ref, state_ref, *rest):
    chosen, (held_ref, arrival, departure) = rest[:-3], rest[-3:]
    members, count = len(chosen), chosen[0].shape[0]
    group_first = lax.axis_index("grp") * members * count
    reads, writes = [], []
    for step in range(members):
        receiver, _ = meeting(step)
        for b in range(count):
            prompt = prompt_ref[group_first + receiver * count + b]
            slot = step * count + b
            reads.append(
                pltpu.make_async_copy(state_ref.at[prompt], held_ref.at[slot], arrival.at[slot])
            )
            writes.append(
                pltpu.make_async_copy(held_ref.at[slot], chosen[step].at[b], departure.at[slot])
            )
    for read in reads:
        read.start()
    for read, write in zip(reads, writes):
        read.wait()
        write.start()
    for write in writes:
        write.wait()


def second_kernel(members, valid_ref, *refs):
    row_hbm, (beta_hbm, inverse_hbm), refs = refs[:7], refs[7:9], refs[9:]
    state_hbm, out_hbm, refs = refs[:members], refs[members : members + 4], refs[members + 4 :]
    rows_ref, beta_ref, inverse_ref, state_ref, out_ref, beta_grad_ref, arrival, departure = refs
    branch = pl.program_id(0)
    heads, tokens, _ = inverse_ref.shape
    head_dim = rows_ref.shape[2] // heads
    here = state_ref.shape[1]
    parts = halves(heads, head_dim)
    pairs = []
    for numbers, lanes in parts:
        for i, ref in enumerate(row_hbm):
            pairs.append((ref.at[branch, :, lanes], rows_ref.at[i, :, lanes]))
        some = pl.ds(numbers[0], len(numbers))
        pairs.append((inverse_hbm.at[branch, some], inverse_ref.at[some]))
    for i in range(members):
        _, sender = meeting(i)
        pairs.append((state_hbm[i].at[branch], state_ref.at[sender]))
    pairs.append((beta_hbm.at[branch], beta_ref))
    arriving = start_all(pairs, arrival)
    each = len(row_hbm) + 1

    valid = valid_ref[own_branch(pl.num_programs(0)) + branch]
    row, col = iota2((tokens, tokens), 0), iota2((tokens, tokens), 1)
    tri = (row >= col).astype(BF16)
    later = (row <= col).astype(BF16)
    later = jnp.concatenate([later, later], axis=1)
    keep = iota2((tokens, 1), 0) < valid
    rows, own_rows = [], []
    for p, (numbers, _) in enumerate(parts):
        for copy in arriving[each * p : each * (p + 1)]:
            copy.wait()
        for j in numbers:
            own_rows.append([rows_ref[i, :, head_lanes(j, head_dim)] for i in range(len(row_hbm))])
            query, key, _, decay = own_rows[j][:4]
            rows.append(decayed_rows(query, key, decay, valid, tri))
    for copy in arriving[each * len(parts) :]:
        copy.wait()
    logits = beta_ref[...].astype(F32).T
    betas = jax.nn.sigmoid(logits) * keep.astype(F32)
    every = range(heads)
    state = [state_ref[j // here, j % here] for j in every]
    target = [
        own_rows[j][2].astype(F32)
        - dot3(split(rows[j]["key_forward"] * rows[j]["start"]), split(state[j]))
        for j in every
    ]
    update = [
        split(
            dot3(
                split(betas[:, j : j + 1] * target[j]),
                (inverse_ref[j, :, :tokens], inverse_ref[j, :, tokens:]),
                TN,
            )
        )
        for j in every
    ]
    against = [stack(u, split(x.T), 1) for u, x in zip(update, state)]
    products = []
    for j in every:
        grad, high, low = own_rows[j][4:]
        grad = jnp.where(keep, grad, jnp.zeros_like(grad))
        high = jnp.concatenate([grad, -high], axis=0)
        total = dot(high, against[j][0]) + dot(high, against[j][1])
        products.append((total[:tokens], total[tokens:] - dot(low, against[j][0])))
    attend_grad = [jnp.where(row >= col, p[0][:, :tokens], 0.0) for p in products]
    coupling_grad = [jnp.where(row > col, p[1][:, :tokens], 0.0) for p in products]
    both = [split(jnp.concatenate([p, c], axis=0)) for p, c in zip(attend_grad, coupling_grad)]
    through_rows = [dot3(x, split(r["key_earlier"])) for x, r in zip(both, rows)]
    earlier = [
        dot3(x, split(jnp.concatenate([r["query_forward"], r["key_forward"]], axis=0)), TN)
        for x, r in zip(both, rows)
    ]
    strengths = jnp.zeros(logits.shape, F32)
    leaving = []
    for numbers, lanes in parts:
        for j in numbers:
            r = rows[j]
            query_forward = products[j][0][:, tokens:] * r["start"] + through_rows[j][:tokens]
            key_forward = products[j][1][:, tokens:] * r["start"] + through_rows[j][tokens:]
            query_unit_grad = query_forward * (r["grow"] * head_dim**-0.5)
            key_later = key_forward * r["grow"]
            key_before = earlier[j] * r["shrink"]
            key_unit_grad = key_later + key_before
            decay_step = r["unit_query"] * query_unit_grad + r["unit_key"] * (
                key_later - key_before
            )
            decay_grad = dot(later, jnp.concatenate(split(decay_step), axis=0))
            decay_grad = jnp.where(keep, decay_grad, 0.0)
            along = jnp.sum(r["unit_query"] * query_unit_grad, axis=1, keepdims=True)
            query_grad = r["query_scale"] * (query_unit_grad - r["unit_query"] * along)
            along = jnp.sum(r["unit_key"] * key_unit_grad, axis=1, keepdims=True)
            key_grad = r["key_scale"] * (key_unit_grad - r["unit_key"] * along)
            for i, grad in enumerate((query_grad, key_grad, decay_grad)):
                out_ref[i, :, head_lanes(j, head_dim)] = grad.astype(BF16)
            strength = jnp.sum(
                jnp.where(row == col, -products[j][1][:, :tokens], 0.0), axis=1, keepdims=True
            )
            strengths = jnp.where(iota2(logits.shape, 1) == j, strength, strengths)
        for i in range(3):
            copy = pltpu.make_async_copy(
                out_ref.at[i, :, lanes], out_hbm[i].at[branch, :, lanes], departure.at[len(leaving)]
            )
            copy.start()
            leaving.append(copy)
    beta_grad_ref[...] = (strengths * jnp.exp(-logits)).T.astype(BF16)
    copy = pltpu.make_async_copy(beta_grad_ref, out_hbm[3].at[branch], departure.at[len(leaving)])
    copy.start()
    leaving.append(copy)
    for copy in leaving:
        copy.wait()


def sum_kernel(prompt_ref, coded_ref, out_ref, total_ref):
    total_ref[...] = jnp.zeros_like(total_ref)

    def add(branch, carry):
        total_ref[prompt_ref[branch]] += decode(coded_ref[branch])
        return carry

    lax.fori_loop(0, coded_ref.shape[0], add, 0, unroll=8)
    out_ref[...] = encode(total_ref[...])


def spread_kernel(*refs):
    pieces, (out_hbm, out_ref, departure) = refs[:-3], refs[-3:]
    chips = len(pieces) // 2
    prompts = out_ref.shape[0]
    parts = next(n for n in (4, 2, 1) if prompts % n == 0)
    size = prompts // parts
    leaving = []
    for p in range(parts):
        some = pl.ds(p * size, size)
        for i, piece in enumerate(pieces):
            place = source(-i % chips, chips) ^ (i // chips)
            out_ref[some, :, pl.ds(place, 1)] = decode(piece[some])[:, :, None]
        leaving.append(pltpu.make_async_copy(out_ref.at[some], out_hbm.at[some], departure.at[p]))
        leaving[p].start()
    for copy in leaving:
        copy.wait()


def source(step, chips):
    me = lax.axis_index("grp")
    if chips & (chips - 1) == 0:
        return me ^ (2 * step)
    return (me // 2 - step + chips) % chips * 2 + me % 2


def gather_pieces(piece, beside):
    size = lax.axis_size("grp")
    chips = size // 2
    power = chips & (chips - 1) == 0
    pieces = [piece]
    for step in reversed(range(1, chips)):
        other = [((c ^ step) if power else (c + step) % chips) for c in range(chips)]
        moves = [(2 * c + core, 2 * other[c] + core) for c in range(chips) for core in range(2)]
        pieces.append(lax.ppermute(piece, "grp", moves))
    swap = [(i, i ^ 1) for i in range(size)]
    swapped = lax.ppermute(piece, "grp", swap)
    pieces, swapped, _ = lax.optimization_barrier((pieces, swapped, beside))
    return pieces + [swapped] + [lax.ppermute(x, "grp", swap) for x in pieces[1:]]


def moves_at(step, members):
    if members & (members - 1) == 0:
        return [(m, m ^ step) for m in range(members)]
    return [(m, (m + step) % members) for m in range(members)]


def meeting(step):
    members = lax.axis_size("head")
    me = lax.axis_index("head")
    if members & (members - 1) == 0:
        return me ^ step, me ^ step
    return (me + step) % members, (me - step + members) % members


def per_device(
    query_rows,
    key_rows,
    value_rows,
    log_decay,
    beta_logit,
    out_grad,
    fork_state,
    branch_prompt,
    valid_len,
):
    count, tokens, width = query_rows.shape
    prompts, heads_here, head_dim, _ = fork_state.shape
    members = lax.axis_size("head")
    groups = lax.axis_size("grp")
    heads = members * heads_here
    piece_rows = head_dim // groups
    params = pltpu.CompilerParams(vmem_limit_bytes=62 * 2**20)
    small = pltpu.CompilerParams(vmem_limit_bytes=16 * 2**20)
    rows_type = jax.ShapeDtypeStruct(query_rows.shape, BF16)
    units = count * heads * tokens * tokens * head_dim
    betas = jnp.swapaxes(beta_logit, 1, 2)
    anywhere = pl.BlockSpec(memory_space=pl.ANY)

    parts = len(halves(heads, head_dim))
    value_grad, value_low, inverse, coded = pl.pallas_call(
        functools.partial(first_kernel, 16),
        grid_spec=pltpu.PrefetchScalarGridSpec(
            num_scalar_prefetch=1,
            grid=(count,),
            in_specs=[anywhere] * 5,
            out_specs=[anywhere] * 4,
            scratch_shapes=[
                pltpu.VMEM((4, tokens, width), BF16),
                pltpu.VMEM((heads, tokens), BF16),
                pltpu.VMEM((tokens, width), BF16),
                pltpu.VMEM((tokens, width), BF16),
                pltpu.VMEM((heads, tokens, 2 * tokens), BF16),
                pltpu.VMEM((groups, heads, piece_rows, head_dim), BF16),
                pltpu.SemaphoreType.DMA((3 * parts + 2,)),
                pltpu.SemaphoreType.DMA((3 + parts,)),
            ],
        ),
        out_shape=[
            rows_type,
            rows_type,
            jax.ShapeDtypeStruct((count, heads, tokens, 2 * tokens), BF16),
            jax.ShapeDtypeStruct((groups, count * heads, piece_rows, head_dim), BF16),
        ],
        compiler_params=params,
        cost_estimate=pl.CostEstimate(flops=100 * units, bytes_accessed=2**23, transcendentals=0),
        name="state_independent",
    )(valid_len, query_rows, key_rows, log_decay, out_grad, betas)

    states_after, coded = lax.optimization_barrier((fork_state, coded))
    states = pl.pallas_call(
        choose_kernel,
        grid_spec=pltpu.PrefetchScalarGridSpec(
            num_scalar_prefetch=1,
            grid=(1,),
            in_specs=[anywhere],
            out_specs=[anywhere] * members,
            scratch_shapes=[
                pltpu.VMEM((members * count, heads_here, head_dim, head_dim), F32),
                pltpu.SemaphoreType.DMA((members * count,)),
                pltpu.SemaphoreType.DMA((members * count,)),
            ],
        ),
        out_shape=[jax.ShapeDtypeStruct((count, heads_here, head_dim, head_dim), F32)] * members,
        compiler_params=params,
        name="choose_states",
    )(branch_prompt, states_after)
    states = [states[0]] + [
        lax.ppermute(states[step], "head", moves_at(step, members)) for step in range(1, members)
    ]

    coded = (
        coded.reshape(groups, count, members, heads_here, piece_rows, head_dim)
        .transpose(0, 2, 1, 3, 4, 5)
        .reshape(groups * members, count, heads_here, piece_rows, head_dim)
    )
    arrived = lax.all_to_all(coded, ("grp", "head"), 0, 0, tiled=True)

    query_grad, key_grad, decay_grad, beta_grad = pl.pallas_call(
        functools.partial(second_kernel, members),
        grid_spec=pltpu.PrefetchScalarGridSpec(
            num_scalar_prefetch=1,
            grid=(count,),
            in_specs=[anywhere] * (9 + members),
            out_specs=[anywhere] * 4,
            scratch_shapes=[
                pltpu.VMEM((7, tokens, width), BF16),
                pltpu.VMEM((heads, tokens), BF16),
                pltpu.VMEM((heads, tokens, 2 * tokens), BF16),
                pltpu.VMEM((members, heads_here, head_dim, head_dim), F32),
                pltpu.VMEM((3, tokens, width), BF16),
                pltpu.VMEM((heads, tokens), BF16),
                pltpu.SemaphoreType.DMA((8 * parts + members + 1,)),
                pltpu.SemaphoreType.DMA((3 * parts + 1,)),
            ],
        ),
        out_shape=[rows_type] * 3 + [jax.ShapeDtypeStruct((count, heads, tokens), BF16)],
        compiler_params=params,
        cost_estimate=pl.CostEstimate(flops=120 * units, bytes_accessed=2**23, transcendentals=0),
        name="state_dependent",
    )(
        valid_len,
        query_rows,
        key_rows,
        value_rows,
        log_decay,
        out_grad,
        value_grad,
        value_low,
        betas,
        inverse,
        *states,
    )

    piece_shape = (prompts, heads_here, piece_rows, head_dim)
    branches = groups * members * count
    whole = pl.BlockSpec(memory_space=pltpu.VMEM)
    scalars = pl.BlockSpec(memory_space=pltpu.SMEM)
    piece = pl.pallas_call(
        sum_kernel,
        in_specs=[scalars, whole],
        out_specs=whole,
        out_shape=jax.ShapeDtypeStruct(piece_shape, BF16),
        scratch_shapes=[pltpu.VMEM(piece_shape, F32)],
        compiler_params=small,
        name="sum_by_prompt",
    )(branch_prompt, arrived.reshape(branches, heads_here, piece_rows, head_dim))
    pieces = gather_pieces(piece, query_grad)
    fork_shape = (prompts, heads_here, groups, piece_rows, head_dim)
    grad_fork = pl.pallas_call(
        spread_kernel,
        in_specs=[whole] * len(pieces),
        out_specs=anywhere,
        out_shape=jax.ShapeDtypeStruct(fork_shape, F32),
        scratch_shapes=[pltpu.VMEM(fork_shape, F32), pltpu.SemaphoreType.DMA((4,))],
        compiler_params=small,
        name="spread_pieces",
    )(*pieces)
    return (
        query_grad,
        key_grad,
        value_grad,
        decay_grad,
        jnp.swapaxes(beta_grad, 1, 2),
        grad_fork.reshape(fork_state.shape),
    )


def solution(mesh):
    rows = P(("grp", "head"), None, None)
    state = P(None, "head", None, None)
    return jax.shard_map(
        per_device,
        mesh=mesh,
        in_specs=(rows, rows, rows, rows, rows, rows, state, P(), P()),
        out_specs=(rows, rows, rows, rows, rows, state),
        check_vma=False,
    )
```

```python
import functools

import jax
import jax.numpy as jnp
from jax import lax
from jax.experimental import pallas as pl
from jax.experimental.pallas import tpu as pltpu
from jax.sharding import PartitionSpec as P

HIGH = lax.Precision.HIGH
NN = ((1,), (0,))
NT = ((1,), (1,))
TN = ((0,), (0,))
F32 = jnp.float32
BF16 = jnp.bfloat16


def dot(a, b, dims=NN, precision=None):
    return lax.dot_general(
        a, b, (dims, ((), ())), preferred_element_type=F32, precision=precision
    )


def split(x):
    high = x.astype(BF16)
    return high, (x - high.astype(F32)).astype(BF16)


def encode(x):
    return (x * x * x * jnp.abs(x)).astype(BF16)


def decode(y):
    wide = y.astype(F32)
    root = lax.rsqrt(lax.rsqrt(jnp.abs(wide)))
    return jnp.where(wide < 0, -root, root)


def iota2(shape, axis):
    return lax.broadcasted_iota(jnp.int32, shape, axis)


def dot3(a, b, dims=NN):
    return dot(a[0], b[0], dims) + dot(a[1], b[0], dims) + dot(a[0], b[1], dims)


def stack(a, b, axis):
    return tuple(jnp.concatenate([x, y], axis=axis) for x, y in zip(a, b))


def unit_upper_inverse(matrices, width):
    size = matrices[0].shape[0]
    blocks = size // width
    row, col = iota2((size, size), 0), iota2((size, size), 1)
    on_block = row // width == col // width
    lane = iota2((8, size), 1)
    identity = (iota2((width, size), 0) == iota2((width, size), 1) % width).astype(F32)
    inverses = []
    for a in matrices:
        compact = jnp.sum(jnp.where(on_block, a, 0.0).reshape(blocks, width, size), axis=0)
        slabs = [compact[i : i + 8] for i in range(0, width, 8)]
        result = [identity[i : i + 8] for i in range(0, width, 8)]
        for m in reversed(range(1, width)):
            source = result[m // 8][m % 8 : m % 8 + 1]
            for i in range((m - 1) // 8 + 1):
                column = jnp.take_along_axis(slabs[i], lane // width * width + m, axis=1)
                result[i] = result[i] - column * source
        inverses.append(jnp.where(on_block, jnp.concatenate(result * blocks, axis=0), 0.0))
    while width * 2 < size:
        upper = (row // (2 * width) == col // (2 * width)) & (row // width < col // width)
        parts = [split(d) for d in inverses]
        inner = [dot3(split(jnp.where(upper, a, 0.0)), d) for a, d in zip(matrices, parts)]
        inverses = [d - dot3(p, split(x)) for d, p, x in zip(inverses, parts, inner)]
        width *= 2
    results = []
    first = [split(d[:width, :width]) for d in inverses]
    second = [split(d[width:, width:]) for d in inverses]
    inner = [dot3(split(a[:width, width:]), d) for a, d in zip(matrices, second)]
    corner = [dot3(d, split(x)) for d, x in zip(first, inner)]
    for d, x in zip(inverses, corner):
        top = jnp.concatenate([d[:width, :width], -x], axis=1)
        results.append(jnp.concatenate([top, d[width:]], axis=0))
    return results


def decayed_rows(query_in, key_in, decay_in, valid, tri):
    tokens, head_dim = query_in.shape
    row = iota2((tokens, 1), 0)
    query = query_in.astype(F32)
    key = key_in.astype(F32)
    query_scale = lax.rsqrt(jnp.sum(query * query, axis=1, keepdims=True) + 1e-06)
    key_scale = lax.rsqrt(jnp.sum(key * key, axis=1, keepdims=True) + 1e-06)
    unit_query = query * query_scale
    unit_key = key * key_scale
    decay = jnp.where(row < valid, decay_in, jnp.zeros_like(decay_in))
    cumulative = dot(tri, decay)
    middle = cumulative[tokens // 2 - 1 : tokens // 2]
    cumulative = cumulative - middle
    grow = jnp.exp(cumulative)
    shrink = jnp.exp(-cumulative)
    return dict(
        unit_query=unit_query,
        unit_key=unit_key,
        query_scale=query_scale,
        key_scale=key_scale,
        grow=grow,
        shrink=shrink,
        start=jnp.exp(middle),
        key_forward=unit_key * grow,
        key_earlier=unit_key * shrink,
        query_forward=unit_query * (grow * head_dim**-0.5),
    )


def own_branch(count):
    place = lax.axis_index("grp") * lax.axis_size("head") + lax.axis_index("head")
    return place * count


def halves(heads, head_dim):
    parts = 2 if heads % 2 == 0 else 1
    size = heads // parts
    numbers = [range(p * size, (p + 1) * size) for p in range(parts)]
    return [(list(n), slice(n[0] * head_dim, (n[-1] + 1) * head_dim)) for n in numbers]


def start_all(pairs, done, first=0):
    copies = [pltpu.make_async_copy(a, b, done.at[first + i]) for i, (a, b) in enumerate(pairs)]
    for copy in copies:
        copy.start()
    return copies


def head_lanes(j, head_dim):
    return slice(j * head_dim, (j + 1) * head_dim)


def first_kernel(
    width,
    valid_ref,
    query_hbm,
    key_hbm,
    decay_hbm,
    grad_hbm,
    beta_hbm,
    value_grad_hbm,
    value_low_hbm,
    inverse_hbm,
    coded_hbm,
    rows_ref,
    beta_ref,
    value_grad_ref,
    value_low_ref,
    inverse_ref,
    coded_ref,
    arrival,
    departure,
):
    branch = pl.program_id(0)
    heads, tokens, _ = inverse_ref.shape
    pieces, _, piece_rows, head_dim = coded_ref.shape
    parts = halves(heads, head_dim)
    inputs = (query_hbm, key_hbm, decay_hbm)

    def fetch(p):
        lanes = parts[p][1]
        return start_all(
            [(x.at[branch, :, lanes], rows_ref.at[i, :, lanes]) for i, x in enumerate(inputs)],
            arrival,
            3 * p,
        )

    arriving = fetch(0)
    valid = valid_ref[own_branch(pl.num_programs(0)) + branch]
    row, col = iota2((tokens, tokens), 0), iota2((tokens, tokens), 1)
    tri = (row >= col).astype(BF16)
    keep = iota2((tokens, 1), 0) < valid
    lane_keep = iota2((1, tokens), 1) < valid
    rows, across, scores = [], [], []
    for p, (numbers, _) in enumerate(parts):
        for copy in arriving:
            copy.wait()
        if p + 1 < len(parts):
            arriving = fetch(p + 1)
        else:
            arriving = start_all(
                [(beta_hbm.at[branch], beta_ref), (grad_hbm.at[branch], rows_ref.at[3])],
                arrival,
                3 * len(parts),
            )
        fresh = [
            decayed_rows(*(rows_ref[i, :, head_lanes(j, head_dim)] for i in range(3)), valid, tri)
            for j in numbers
        ]
        turned = [
            split(jnp.concatenate([r["key_forward"], r["query_forward"]], axis=0).T) for r in fresh
        ]
        scores += [dot3(split(r["key_earlier"]), x) for r, x in zip(fresh, turned)]
        rows += fresh
        across += turned
    for copy in arriving:
        copy.wait()
    out_grad = []
    for j in range(heads):
        grad = rows_ref[3, :, head_lanes(j, head_dim)]
        out_grad.append(jnp.where(keep, grad, jnp.zeros_like(grad)))
    flat_betas = jax.nn.sigmoid(beta_ref[...].astype(F32)) * lane_keep.astype(F32)
    betas = flat_betas.T
    every = range(heads)
    beta = [betas[:, j : j + 1] for j in every]
    coupling = [
        jnp.where(row < col, s[:, :tokens] * flat_betas[j : j + 1], 0.0)
        for j, s in enumerate(scores)
    ]
    attend = [split(jnp.where(row <= col, s[:, tokens:], 0.0)) for s in scores]
    inverse = [split(x) for x in unit_upper_inverse(coupling, width)]
    for j in every:
        inverse_ref[j] = jnp.concatenate(inverse[j], axis=1)
    leaving = start_all([(inverse_ref, inverse_hbm.at[branch])], departure)
    update_grad = [split(dot(p[0], g) + dot(p[1], g)) for p, g in zip(attend, out_grad)]
    value_grad = [split(b * dot3(d, u)) for b, d, u in zip(beta, inverse, update_grad)]
    for j in every:
        value_grad_ref[:, head_lanes(j, head_dim)] = value_grad[j][0]
        value_low_ref[:, head_lanes(j, head_dim)] = value_grad[j][1]
    leaving += start_all(
        [
            (value_grad_ref, value_grad_hbm.at[branch]),
            (value_low_ref, value_low_hbm.at[branch]),
        ],
        departure,
        1,
    )
    for p, (numbers, _) in enumerate(parts):
        for j in numbers:
            high = jnp.concatenate([-value_grad[j][0], out_grad[j]], axis=0)
            start = jnp.broadcast_to(rows[j]["start"], (8, head_dim)).T[:, :1]
            state_grad = start * (
                dot(across[j][0], high)
                + dot(across[j][1], high)
                - dot(across[j][0][:, :tokens], value_grad[j][1])
            )
            coded_ref[:, j] = encode(state_grad).reshape(pieces, piece_rows, head_dim)
        first, size = numbers[0], len(numbers)
        copy = pltpu.make_async_copy(
            coded_ref.at[:, pl.ds(first, size)],
            coded_hbm.at[:, pl.ds(branch * heads + first, size)],
            departure.at[3 + p],
        )
        copy.start()
        leaving.append(copy)
    for copy in leaving:
        copy.wait()


def choose_kernel(prompt_ref, state_ref, *rest):
    chosen, (held_ref, arrival, departure) = rest[:-3], rest[-3:]
    members, count = len(chosen), chosen[0].shape[0]
    group_first = lax.axis_index("grp") * members * count
    reads, writes = [], []
    for step in reversed(range(members)):
        receiver, _ = meeting(step)
        for b in range(count):
            prompt = prompt_ref[group_first + receiver * count + b]
            slot = step * count + b
            reads.append(
                pltpu.make_async_copy(state_ref.at[prompt], held_ref.at[slot], arrival.at[slot])
            )
            writes.append(
                pltpu.make_async_copy(held_ref.at[slot], chosen[step].at[b], departure.at[slot])
            )
    for read in reads:
        read.start()
    for read, write in zip(reads, writes):
        read.wait()
        write.start()
    for write in writes:
        write.wait()


def second_kernel(members, valid_ref, *refs):
    row_hbm, (beta_hbm, inverse_hbm), refs = refs[:7], refs[7:9], refs[9:]
    state_hbm, out_hbm, refs = refs[:members], refs[members : members + 4], refs[members + 4 :]
    rows_ref, beta_ref, inverse_ref, state_ref, out_ref, beta_grad_ref, arrival, departure = refs
    branch = pl.program_id(0)
    heads, tokens, _ = inverse_ref.shape
    head_dim = rows_ref.shape[2] // heads
    here = state_ref.shape[1]
    parts = halves(heads, head_dim)
    pairs = []
    for numbers, lanes in parts:
        for i, ref in enumerate(row_hbm):
            pairs.append((ref.at[branch, :, lanes], rows_ref.at[i, :, lanes]))
        some = pl.ds(numbers[0], len(numbers))
        pairs.append((inverse_hbm.at[branch, some], inverse_ref.at[some]))
    for i in range(members):
        _, sender = meeting(i)
        pairs.append((state_hbm[i].at[branch], state_ref.at[sender]))
    pairs.append((beta_hbm.at[branch], beta_ref))
    arriving = start_all(pairs, arrival)
    each = len(row_hbm) + 1

    valid = valid_ref[own_branch(pl.num_programs(0)) + branch]
    row, col = iota2((tokens, tokens), 0), iota2((tokens, tokens), 1)
    tri = (row >= col).astype(BF16)
    later = (row <= col).astype(BF16)
    later = jnp.concatenate([later, later], axis=1)
    keep = iota2((tokens, 1), 0) < valid
    rows, own_rows = [], []
    for p, (numbers, _) in enumerate(parts):
        for copy in arriving[each * p : each * (p + 1)]:
            copy.wait()
        for j in numbers:
            own_rows.append([rows_ref[i, :, head_lanes(j, head_dim)] for i in range(len(row_hbm))])
            query, key, _, decay = own_rows[j][:4]
            rows.append(decayed_rows(query, key, decay, valid, tri))
    for copy in arriving[each * len(parts) :]:
        copy.wait()
    logits = beta_ref[...].astype(F32).T
    betas = jax.nn.sigmoid(logits) * keep.astype(F32)
    every = range(heads)
    state = [state_ref[j // here, j % here] for j in every]
    target = [
        own_rows[j][2].astype(F32)
        - dot3(split(rows[j]["key_forward"] * rows[j]["start"]), split(state[j]))
        for j in every
    ]
    update = [
        split(
            dot3(
                split(betas[:, j : j + 1] * target[j]),
                (inverse_ref[j, :, :tokens], inverse_ref[j, :, tokens:]),
                TN,
            )
        )
        for j in every
    ]
    against = [stack(u, split(x.T), 1) for u, x in zip(update, state)]
    products = []
    for j in every:
        grad, high, low = own_rows[j][4:]
        grad = jnp.where(keep, grad, jnp.zeros_like(grad))
        high = jnp.concatenate([grad, -high], axis=0)
        total = dot(high, against[j][0]) + dot(high, against[j][1])
        products.append((total[:tokens], total[tokens:] - dot(low, against[j][0])))
    attend_grad = [jnp.where(row >= col, p[0][:, :tokens], 0.0) for p in products]
    coupling_grad = [jnp.where(row > col, p[1][:, :tokens], 0.0) for p in products]
    both = [split(jnp.concatenate([p, c], axis=0)) for p, c in zip(attend_grad, coupling_grad)]
    through_rows = [dot3(x, split(r["key_earlier"])) for x, r in zip(both, rows)]
    earlier = [
        dot3(x, split(jnp.concatenate([r["query_forward"], r["key_forward"]], axis=0)), TN)
        for x, r in zip(both, rows)
    ]
    strengths = jnp.zeros(logits.shape, F32)
    leaving = []
    for numbers, lanes in parts:
        for j in numbers:
            r = rows[j]
            query_forward = products[j][0][:, tokens:] * r["start"] + through_rows[j][:tokens]
            key_forward = products[j][1][:, tokens:] * r["start"] + through_rows[j][tokens:]
            query_unit_grad = query_forward * (r["grow"] * head_dim**-0.5)
            key_later = key_forward * r["grow"]
            key_before = earlier[j] * r["shrink"]
            key_unit_grad = key_later + key_before
            decay_step = r["unit_query"] * query_unit_grad + r["unit_key"] * (
                key_later - key_before
            )
            decay_grad = dot(later, jnp.concatenate(split(decay_step), axis=0))
            decay_grad = jnp.where(keep, decay_grad, 0.0)
            along = jnp.sum(r["unit_query"] * query_unit_grad, axis=1, keepdims=True)
            query_grad = r["query_scale"] * (query_unit_grad - r["unit_query"] * along)
            along = jnp.sum(r["unit_key"] * key_unit_grad, axis=1, keepdims=True)
            key_grad = r["key_scale"] * (key_unit_grad - r["unit_key"] * along)
            for i, grad in enumerate((query_grad, key_grad, decay_grad)):
                out_ref[i, :, head_lanes(j, head_dim)] = grad.astype(BF16)
            strength = jnp.sum(
                jnp.where(row == col, -products[j][1][:, :tokens], 0.0), axis=1, keepdims=True
            )
            strengths = jnp.where(iota2(logits.shape, 1) == j, strength, strengths)
        for i in range(3):
            copy = pltpu.make_async_copy(
                out_ref.at[i, :, lanes], out_hbm[i].at[branch, :, lanes], departure.at[len(leaving)]
            )
            copy.start()
            leaving.append(copy)
    beta_grad_ref[...] = (strengths * jnp.exp(-logits)).T.astype(BF16)
    copy = pltpu.make_async_copy(beta_grad_ref, out_hbm[3].at[branch], departure.at[len(leaving)])
    copy.start()
    leaving.append(copy)
    for copy in leaving:
        copy.wait()


def sum_kernel(prompt_ref, coded_ref, out_ref, total_ref):
    total_ref[...] = jnp.zeros_like(total_ref)

    def add(branch, carry):
        total_ref[prompt_ref[branch]] += decode(coded_ref[branch])
        return carry

    lax.fori_loop(0, coded_ref.shape[0], add, 0, unroll=8)
    out_ref[...] = encode(total_ref[...])


def spread_kernel(*refs):
    pieces, (out_hbm, out_ref, departure) = refs[:-3], refs[-3:]
    chips = len(pieces) // 2
    prompts = out_ref.shape[0]
    parts = next(n for n in (4, 2, 1) if prompts % n == 0)
    size = prompts // parts
    leaving = []
    for p in range(parts):
        some = pl.ds(p * size, size)
        for i, piece in enumerate(pieces):
            place = source(-i % chips, chips) ^ (i // chips)
            out_ref[some, :, pl.ds(place, 1)] = decode(piece[some])[:, :, None]
        leaving.append(pltpu.make_async_copy(out_ref.at[some], out_hbm.at[some], departure.at[p]))
        leaving[p].start()
    for copy in leaving:
        copy.wait()


def source(step, chips):
    me = lax.axis_index("grp")
    if chips & (chips - 1) == 0:
        return me ^ (2 * step)
    return (me // 2 - step + chips) % chips * 2 + me % 2


def gather_pieces(piece, beside):
    size = lax.axis_size("grp")
    chips = size // 2
    power = chips & (chips - 1) == 0
    pieces = [piece]
    for step in reversed(range(1, chips)):
        other = [((c ^ step) if power else (c + step) % chips) for c in range(chips)]
        moves = [(2 * c + core, 2 * other[c] + core) for c in range(chips) for core in range(2)]
        pieces.append(lax.ppermute(piece, "grp", moves))
    swap = [(i, i ^ 1) for i in range(size)]
    swapped = lax.ppermute(piece, "grp", swap)
    pieces, swapped, _ = lax.optimization_barrier((pieces, swapped, beside))
    return pieces + [swapped] + [lax.ppermute(x, "grp", swap) for x in pieces[1:]]


def moves_at(step, members):
    if members & (members - 1) == 0:
        return [(m, m ^ step) for m in range(members)]
    return [(m, (m + step) % members) for m in range(members)]


def meeting(step):
    members = lax.axis_size("head")
    me = lax.axis_index("head")
    if members & (members - 1) == 0:
        return me ^ step, me ^ step
    return (me + step) % members, (me - step + members) % members


def per_device(
    query_rows,
    key_rows,
    value_rows,
    log_decay,
    beta_logit,
    out_grad,
    fork_state,
    branch_prompt,
    valid_len,
):
    count, tokens, width = query_rows.shape
    prompts, heads_here, head_dim, _ = fork_state.shape
    members = lax.axis_size("head")
    groups = lax.axis_size("grp")
    heads = members * heads_here
    piece_rows = head_dim // groups
    params = pltpu.CompilerParams(vmem_limit_bytes=62 * 2**20)
    small = pltpu.CompilerParams(vmem_limit_bytes=16 * 2**20)
    rows_type = jax.ShapeDtypeStruct(query_rows.shape, BF16)
    units = count * heads * tokens * tokens * head_dim
    betas = jnp.swapaxes(beta_logit, 1, 2)
    anywhere = pl.BlockSpec(memory_space=pl.ANY)

    parts = len(halves(heads, head_dim))
    value_grad, value_low, inverse, coded = pl.pallas_call(
        functools.partial(first_kernel, 16),
        grid_spec=pltpu.PrefetchScalarGridSpec(
            num_scalar_prefetch=1,
            grid=(count,),
            in_specs=[anywhere] * 5,
            out_specs=[anywhere] * 4,
            scratch_shapes=[
                pltpu.VMEM((4, tokens, width), BF16),
                pltpu.VMEM((heads, tokens), BF16),
                pltpu.VMEM((tokens, width), BF16),
                pltpu.VMEM((tokens, width), BF16),
                pltpu.VMEM((heads, tokens, 2 * tokens), BF16),
                pltpu.VMEM((groups, heads, piece_rows, head_dim), BF16),
                pltpu.SemaphoreType.DMA((3 * parts + 2,)),
                pltpu.SemaphoreType.DMA((3 + parts,)),
            ],
        ),
        out_shape=[
            rows_type,
            rows_type,
            jax.ShapeDtypeStruct((count, heads, tokens, 2 * tokens), BF16),
            jax.ShapeDtypeStruct((groups, count * heads, piece_rows, head_dim), BF16),
        ],
        compiler_params=params,
        cost_estimate=pl.CostEstimate(flops=100 * units, bytes_accessed=2**23, transcendentals=0),
        name="state_independent",
    )(valid_len, query_rows, key_rows, log_decay, out_grad, betas)

    states_after, coded = lax.optimization_barrier((fork_state, coded))
    states = pl.pallas_call(
        choose_kernel,
        grid_spec=pltpu.PrefetchScalarGridSpec(
            num_scalar_prefetch=1,
            grid=(1,),
            in_specs=[anywhere],
            out_specs=[anywhere] * members,
            scratch_shapes=[
                pltpu.VMEM((members * count, heads_here, head_dim, head_dim), F32),
                pltpu.SemaphoreType.DMA((members * count,)),
                pltpu.SemaphoreType.DMA((members * count,)),
            ],
        ),
        out_shape=[jax.ShapeDtypeStruct((count, heads_here, head_dim, head_dim), F32)] * members,
        compiler_params=params,
        name="choose_states",
    )(branch_prompt, states_after)
    states = list(states)
    for step in reversed(range(1, members)):
        states[step] = lax.ppermute(states[step], "head", moves_at(step, members))

    coded = (
        coded.reshape(groups, count, members, heads_here, piece_rows, head_dim)
        .transpose(0, 2, 1, 3, 4, 5)
        .reshape(groups * members, count, heads_here, piece_rows, head_dim)
    )
    arrived = lax.all_to_all(coded, ("grp", "head"), 0, 0, tiled=True)

    query_grad, key_grad, decay_grad, beta_grad = pl.pallas_call(
        functools.partial(second_kernel, members),
        grid_spec=pltpu.PrefetchScalarGridSpec(
            num_scalar_prefetch=1,
            grid=(count,),
            in_specs=[anywhere] * (9 + members),
            out_specs=[anywhere] * 4,
            scratch_shapes=[
                pltpu.VMEM((7, tokens, width), BF16),
                pltpu.VMEM((heads, tokens), BF16),
                pltpu.VMEM((heads, tokens, 2 * tokens), BF16),
                pltpu.VMEM((members, heads_here, head_dim, head_dim), F32),
                pltpu.VMEM((3, tokens, width), BF16),
                pltpu.VMEM((heads, tokens), BF16),
                pltpu.SemaphoreType.DMA((8 * parts + members + 1,)),
                pltpu.SemaphoreType.DMA((3 * parts + 1,)),
            ],
        ),
        out_shape=[rows_type] * 3 + [jax.ShapeDtypeStruct((count, heads, tokens), BF16)],
        compiler_params=params,
        cost_estimate=pl.CostEstimate(flops=120 * units, bytes_accessed=2**23, transcendentals=0),
        name="state_dependent",
    )(
        valid_len,
        query_rows,
        key_rows,
        value_rows,
        log_decay,
        out_grad,
        value_grad,
        value_low,
        betas,
        inverse,
        *states,
    )

    piece_shape = (prompts, heads_here, piece_rows, head_dim)
    branches = groups * members * count
    whole = pl.BlockSpec(memory_space=pltpu.VMEM)
    scalars = pl.BlockSpec(memory_space=pltpu.SMEM)
    piece = pl.pallas_call(
        sum_kernel,
        in_specs=[scalars, whole],
        out_specs=whole,
        out_shape=jax.ShapeDtypeStruct(piece_shape, BF16),
        scratch_shapes=[pltpu.VMEM(piece_shape, F32)],
        compiler_params=small,
        name="sum_by_prompt",
    )(branch_prompt, arrived.reshape(branches, heads_here, piece_rows, head_dim))
    pieces = gather_pieces(piece, query_grad)
    fork_shape = (prompts, heads_here, groups, piece_rows, head_dim)
    grad_fork = pl.pallas_call(
        spread_kernel,
        in_specs=[whole] * len(pieces),
        out_specs=anywhere,
        out_shape=jax.ShapeDtypeStruct(fork_shape, F32),
        scratch_shapes=[pltpu.VMEM(fork_shape, F32), pltpu.SemaphoreType.DMA((4,))],
        compiler_params=small,
        name="spread_pieces",
    )(*pieces)
    return (
        query_grad,
        key_grad,
        value_grad,
        decay_grad,
        jnp.swapaxes(beta_grad, 1, 2),
        grad_fork.reshape(fork_state.shape),
    )


def solution(mesh):
    rows = P(("grp", "head"), None, None)
    state = P(None, "head", None, None)
    return jax.shard_map(
        per_device,
        mesh=mesh,
        in_specs=(rows, rows, rows, rows, rows, rows, state, P(), P()),
        out_specs=(rows, rows, rows, rows, rows, state),
        check_vma=False,
    )
```
